512 devices in a mesh: row: 16 (over x_lo, y), col: 32 (over z, x_hi, core).
Axes of the slice: x: 4 (x_hi: 2, x_lo: 2; x = x_hi * 2 + x_lo), y: 8, z: 8, core: 2. Of those that a mesh axis runs over, the one named last changes fastest.
Arguments:
- singles: float32 [4096, 384], P(('row', 'col')), may hold values from -6 to 6
- norm_gain: float32 [384], replicated, may hold values from 0.25 to 1.75
- w_query: float32 [384, 384], replicated, may hold values from -0.3125 to 0.3125
- w_key: float32 [384, 384], replicated, may hold values from -0.3125 to 0.3125
- w_value: float32 [384, 384], replicated, may hold values from -0.3125 to 0.3125
- w_gate: float32 [384, 384], replicated, may hold values from -0.3125 to 0.3125
- w_out: float32 [384, 384], replicated, may hold values from -0.3125 to 0.3125
- pair_bias: float32 [16, 4096, 4096], P(None, 'row', 'col'), may hold values from -6 to 256
Outputs:
- updated: float32 [4096, 384], P(('row', 'col'))
The draws below stay inside these ranges and needn't reach their ends.
All inputs are finite; a program needn't handle non-finite values.
Results may differ from the reference program's by a relative error of at most 0.0003.
Values sent between devices are 32-bit elements; how exact they have to be, the bound alone decides.
No kernel may reach another device: no remote copies, remote signals or barrier semaphores. Data moves between devices by JAX's collectives and lax.ppermute only.
A program may use at most 64 MiB of HBM per device.

```python
import jax
import jax.numpy as jnp
from jax import lax

D = 384
HEADS = 16
TOKENS = 4096


def draw_pair_bias(key, part):
    key = jax.random.fold_in(key, 7)
    keys = jax.random.split(key, 7)
    shape = (HEADS, TOKENS, TOKENS)
    return jnp.clip(1.5 * jax.random.normal(keys[6], shape, jnp.float32), -6.0, 6.0)


def levels(stream_key, dims, shards, least, largest):
    def one(dim, parts):
        draws = jax.random.uniform(jax.random.fold_in(jax.random.fold_in(stream_key, 6), dim), (parts,), jnp.float32, least / len(shards), largest / len(shards))
        return jnp.repeat(jnp.exp(draws), dims[dim] // parts).reshape((-1,) + (1,) * (len(dims) - dim - 1))

    level = one(*shards[0])
    for cut in shards[1:]:
        level = level * one(*cut)
    return level


def scatter_about(rng, shape, deviation, most, shards=(), kind=jnp.bfloat16):
    level = levels(rng, shape, shards, -0.22, 0.18) if shards else 1.0
    array = jax.random.normal(rng, shape, jnp.float32) * deviation * level
    return jnp.minimum(jnp.maximum(array, -most), most).astype(kind)


def setup_inputs(seed: int = 0) -> dict:
    streams_of = jax.random.split(jax.random.key(seed), 9)
    singles = scatter_about(streams_of[0], (TOKENS, D), 1.0, 6.0, ((0, 512),), jnp.float32)
    norm_gain = jnp.clip(1.0 + 0.15 * jax.random.normal(streams_of[1], (D,), jnp.float32), 0.25, 1.75)
    w_query = scatter_about(streams_of[2], (D, D), D ** -0.5, 0.3125, (), jnp.float32)
    w_key = scatter_about(streams_of[3], (D, D), D ** -0.5, 0.3125, (), jnp.float32)
    w_value = scatter_about(streams_of[4], (D, D), D ** -0.5, 0.3125, (), jnp.float32)
    w_gate = scatter_about(streams_of[5], (D, D), D ** -0.5, 0.3125, (), jnp.float32)
    w_out = scatter_about(streams_of[6], (D, D), D ** -0.5, 0.3125, (), jnp.float32)
    pair_bias = draw_pair_bias(jax.random.fold_in(streams_of[8], 71), 0)
    return {"singles": singles, "norm_gain": norm_gain, "w_query": w_query, "w_key": w_key, "w_value": w_value, "w_gate": w_gate, "w_out": w_out, "pair_bias": pair_bias}


def layer_norm(rows, gain):
    mean = lax.optimization_barrier(jnp.mean(rows, axis=-1, keepdims=True))
    centred = rows - mean
    var = lax.optimization_barrier(jnp.mean(centred * centred, axis=-1, keepdims=True))
    return centred * lax.rsqrt(var + 1e-05) * gain

def reference(singles, norm_gain, w_query, w_key, w_value, w_gate, w_out, pair_bias):
    exact = lax.Precision.HIGHEST
    normed = layer_norm(singles, norm_gain)
    query = jnp.dot(normed, w_query, precision=exact)
    key = jnp.dot(normed, w_key, precision=exact)
    value = jnp.dot(normed, w_value, precision=exact)
    gate_pre = jnp.dot(normed, w_gate, precision=exact)
    count = singles.shape[0]
    heads = pair_bias.shape[0]
    width = query.shape[1] // heads
    scale = 1.0 / jnp.sqrt(jnp.float32(width))
    q_heads = query.reshape(count, heads, width).transpose(1, 0, 2)
    k_heads = key.reshape(count, heads, width).transpose(1, 0, 2)
    v_heads = value.reshape(count, heads, width).transpose(1, 0, 2)

    def one_head(items):
        q_one, k_one, v_one, b_one = items
        scores = jnp.dot(q_one, k_one.T, precision=exact) * scale + b_one
        top = lax.optimization_barrier(jnp.max(scores, axis=-1, keepdims=True))
        weights = jnp.exp(scores - top)
        total = lax.optimization_barrier(jnp.sum(weights, axis=-1, keepdims=True))
        return jnp.dot(weights, v_one, precision=exact) / total
    attn = lax.map(one_head, (q_heads, k_heads, v_heads, pair_bias))
    attn = attn.transpose(1, 0, 2).reshape(count, heads * width)
    gated = jax.nn.sigmoid(gate_pre) * attn
    return singles + jnp.dot(gated, w_out, precision=exact)
```

```python
import jax
import jax.numpy as jnp
from jax import lax
from jax.sharding import PartitionSpec as P

EXACT = lax.Precision.HIGHEST
ROW, COL, CHIPS = 16, 32, 16
SLICE = 8


def layer_norm(rows, gain):
    mean = jnp.mean(rows, axis=-1, keepdims=True)
    centred = rows - mean
    var = jnp.mean(centred * centred, axis=-1, keepdims=True)
    return centred * lax.rsqrt(var + 1e-05) * gain


def ring(a, b, n):
    return min((a - b) % n, (b - a) % n)


def holders(m):
    z, x_hi = divmod(m, 2)
    x_lo, y = divmod(m, 8)
    zs = sorted(range(8), key=lambda v: (-ring(v, z, 8), v))
    ys = sorted(range(8), key=lambda v: (ring(v, y, 8), v))
    out = [0] * CHIPS
    for z_from, y_to in zip(zs, ys):
        for x_from in range(2):
            out[2 * z_from + x_from] = (x_lo if x_from == x_hi else 1 - x_lo) * 8 + y_to
    return out


HOLDERS = [holders(m) for m in range(CHIPS)]
OVER_M = [[r * COL + 2 * m + k for m in range(CHIPS)] for r in range(ROW) for k in range(2)]
OVER_R = [[r * COL + 2 * m + k for r in HOLDERS[m]] for m in range(CHIPS) for k in range(2)]
SIBLING = [(i, i ^ 1) for i in range(ROW * COL)]


def to_column(flip):
    return [
        (m * COL + 2 * s + (k ^ flip), HOLDERS[m][s] * COL + 2 * m + k)
        for m in range(CHIPS)
        for s in range(CHIPS)
        for k in range(2)
    ]


AXES = ("row", "col")


def exchange(pieces, groups):
    return lax.all_to_all(pieces, AXES, 0, 0, tiled=True, axis_index_groups=groups)


def body(singles, norm_gain, w_query, w_key, w_value, w_gate, w_out, pair_bias):
    dims = singles.shape[1]
    heads, qrows, krows = pair_bias.shape
    width = dims // heads
    core = lax.axis_index("col") % 2
    normed = layer_norm(singles, norm_gain)

    near = lax.ppermute(normed, AXES, to_column(0))
    far = lax.ppermute(normed, AXES, to_column(1))
    halves = pair_bias.reshape(heads, CHIPS, 2, SLICE, krows)
    mine = lax.dynamic_index_in_dim(halves, core, 2, keepdims=False)
    theirs = lax.dynamic_index_in_dim(halves, 1 - core, 2, keepdims=False)
    got = lax.ppermute(theirs, AXES, SIBLING)
    q_in = exchange(jnp.broadcast_to(normed[None], (CHIPS, SLICE, dims)), OVER_M)
    piece = jnp.where(core == 0, jnp.concatenate((near, far)), jnp.concatenate((far, near)))
    k_in = exchange(jnp.broadcast_to(piece[None], (CHIPS, 2 * SLICE, dims)), OVER_R)

    first = jnp.where(core == 0, mine, got)
    second = jnp.where(core == 0, got, mine)
    bias = jnp.concatenate((first, second), axis=-1).reshape(heads, qrows // 2, 2 * krows)

    rows = q_in.reshape(qrows // 2, dims)
    keyside = k_in.reshape(2 * krows, dims)
    query = jnp.dot(rows, w_query, precision=EXACT).reshape(qrows // 2, heads, width)
    key = jnp.dot(keyside, w_key, precision=EXACT).reshape(2 * krows, heads, width)
    value = jnp.dot(keyside, w_value, precision=EXACT).reshape(2 * krows, heads, width)
    scale = 1.0 / jnp.sqrt(jnp.float32(width))
    scores = jnp.einsum("qhd,khd->hqk", query, key, precision=EXACT) * scale + bias
    top = jnp.max(scores, axis=-1)
    weights = jnp.exp(scores - top[:, :, None])
    totals = jnp.sum(weights, axis=-1)
    sums = jnp.einsum("hqk,khd->qhd", weights, value, precision=EXACT).reshape(qrows // 2, dims)
    message = jnp.concatenate((sums, totals.T, top.T), axis=1).reshape(CHIPS, SLICE, dims + 2 * heads)
    parts = exchange(message, OVER_M)
    tops = parts[:, :, dims + heads :]
    share = jnp.exp(tops - jnp.max(tops, axis=0))
    own_totals = jnp.sum(parts[:, :, dims : dims + heads] * share, axis=0)
    own_sums = jnp.sum(parts[:, :, :dims].reshape(CHIPS, SLICE, heads, width) * share[..., None], axis=0)
    attn = (own_sums / own_totals[:, :, None]).reshape(SLICE, dims)
    gate = jax.nn.sigmoid(jnp.dot(normed, w_gate, precision=EXACT))
    return singles + jnp.dot(gate * attn, w_out, precision=EXACT)


def solution(mesh):
    return jax.shard_map(
        body,
        mesh=mesh,
        in_specs=(P(("row", "col"), None), P(), P(), P(), P(), P(), P(), P(None, "row", "col")),
        out_specs=P(("row", "col"), None),
        check_vma=False,
    )
```

```python
import jax
import jax.numpy as jnp
from jax import lax
from jax.experimental import pallas as pl
from jax.experimental.pallas import tpu as pltpu
from jax.sharding import PartitionSpec as P

ROW, COL, CHIPS = 16, 32, 16
SLICE = 8
D, HEADS, WIDTH = 384, 16, 24
TOKENS = 256
SLOT = 32
PAD = HEADS * SLOT
GROUP = 4
GROUPS = HEADS // GROUP
LANES = 128
TOTAL, TOP = WIDTH, WIDTH + 1
F32, BF16 = jnp.float32, jnp.bfloat16


def ring(a, b, n):
    return min((a - b) % n, (b - a) % n)


def holders(m):
    z, x_hi = divmod(m, 2)
    x_lo, y = divmod(m, 8)
    zs = sorted(range(8), key=lambda v: (-ring(v, z, 8), v))
    ys = sorted(range(8), key=lambda v: (ring(v, y, 8), v))
    out = [0] * CHIPS
    for z_from, y_to in zip(zs, ys):
        for x_from in range(2):
            out[2 * z_from + x_from] = (x_lo if x_from == x_hi else 1 - x_lo) * 8 + y_to
    return out


HOLDERS = [holders(m) for m in range(CHIPS)]
OVER_M = [[r * COL + 2 * m + k for m in range(CHIPS)] for r in range(ROW) for k in range(2)]
SIBLING = [(i, i ^ 1) for i in range(ROW * COL)]


MIXED = [[r * COL + 2 * m for m in range(CHIPS)] for r in range(ROW)] + [
    [r * COL + 2 * m + 1 for r in HOLDERS[m]] for m in range(CHIPS)
]
TO_COLUMN = [(m * COL + 2 * s, HOLDERS[m][s] * COL + 2 * m + 1) for m in range(CHIPS) for s in range(CHIPS)]


AXES = ("row", "col")


def exchange(pieces, groups):
    return lax.all_to_all(pieces, AXES, 0, 0, tiled=True, axis_index_groups=groups)


def layer_norm(rows, gain):
    mean = jnp.mean(rows, axis=-1, keepdims=True)
    centred = rows - mean
    var = jnp.mean(centred * centred, axis=-1, keepdims=True)
    return centred * lax.rsqrt(var + 1e-05) * gain


def split(array):
    high = array.astype(BF16)
    return high, (array - high.astype(F32)).astype(BF16)


def dot(a, b):
    return lax.dot_general(a, b, (((1,), (0,)), ((), ())), preferred_element_type=F32)


def dot_t(a, b):
    return lax.dot_general(a, b, (((1,), (1,)), ((), ())), preferred_element_type=F32)


def dot3(a, b):
    return dot(a[0], b[0]) + (dot(a[1], b[0]) + dot(a[0], b[1]))


def iota(shape, dim):
    return lax.broadcasted_iota(jnp.int32, shape, dim)


def spread():
    feature, column = iota((D, PAD), 0), iota((D, PAD), 1)
    head = lax.shift_right_logical(feature * 2731, 16)
    return jnp.where(feature + (SLOT - WIDTH) * head == column, 1.0, 0.0).astype(BF16)


def prepare_kernel(
    core_ref, pair, gain, w_query, w_key, w_value, w_gate, w_out, bias,
    wq_h, wq_l, wkv_h, wkv_l, wo_h, wo_l, gate, gain_out, theirs, held, gain_in, sems,
):
    core = core_ref[0]
    sources = (w_query, w_key, w_value, w_gate, w_out)
    copies = [pltpu.make_async_copy(source, held.at[i], sems.at[i]) for i, source in enumerate(sources)]
    for copy in copies:
        copy.start()
    send = pltpu.make_async_copy(bias.at[:, :, 1 - core], theirs, sems.at[len(sources)])
    send.start()
    fetch = pltpu.make_async_copy(gain, gain_in, sems.at[len(sources) + 1])
    fetch.start()
    place = spread()
    fetch.wait()
    gain_rows = jnp.broadcast_to(gain_in[...], (SLICE, D))
    gain_out[...] = gain_rows
    normed = split(layer_norm(pair[pl.ds(core, 1)].reshape(SLICE, D), gain_rows))
    for i, is_query, first in ((0, True, 0), (1, False, 0), (2, False, 1)):
        copies[i].wait()
        for part, out in zip(split(held[i]), (wq_h, wq_l) if is_query else (wkv_h, wkv_l)):
            wide = dot(part, place).astype(BF16)
            if is_query:
                out[...] = wide
                continue
            for g in range(GROUPS):
                at = (2 * g + first) * LANES
                out[:, at : at + LANES] = wide[:, g * LANES : (g + 1) * LANES]
    copies[3].wait()
    opened = jax.nn.sigmoid(dot3(normed, split(held[3])))
    high = opened.astype(BF16)
    rest = opened - high.astype(F32)
    mid, low = split(rest)
    gate[...] = dot(high, place) + (dot(mid, place) + dot(low, place))
    copies[4].wait()
    out_h, out_l = split(held[4])
    for out, part in ((wo_h, out_h), (wo_l, out_l)):
        out[...] = jnp.zeros((PAD, D), BF16)
        for h in range(HEADS):
            out[SLOT * h : SLOT * h + WIDTH, :] = part[WIDTH * h : WIDTH * (h + 1), :]
    send.wait()


def in_hbm(*arrays):
    return [pltpu.with_memory_space_constraint(array, pltpu.HBM) for array in arrays]


def prepare(core, pair, gain, weights, bias):
    vmem, hbm = pl.BlockSpec(memory_space=pltpu.VMEM), pl.BlockSpec(memory_space=pl.ANY)
    shapes = [(D, PAD)] * 2 + [(D, 2 * PAD)] * 2 + [(PAD, D)] * 2
    tiles = (HEADS, CHIPS, 2, SLICE, LANES)
    return pl.pallas_call(
        prepare_kernel,
        out_shape=[pltpu.VMEM(s, BF16) for s in shapes]
        + [pltpu.VMEM((SLICE, PAD), F32), pltpu.VMEM((SLICE, D), F32), pltpu.VMEM((HEADS, CHIPS, SLICE, LANES), F32)],
        in_specs=[pl.BlockSpec(memory_space=pltpu.SMEM)] + [vmem] + [hbm] * 7,
        out_specs=[vmem] * 9,
        scratch_shapes=[pltpu.VMEM((5, D, D), F32), pltpu.VMEM((1, D), F32), pltpu.SemaphoreType.DMA((7,))],
        compiler_params=pltpu.CompilerParams(vmem_limit_bytes=20 << 20),
        cost_estimate=pl.CostEstimate(flops=2 * 2304 * D * PAD, bytes_accessed=8 << 20, transcendentals=SLICE * D),
        name="prepare",
    )(core.reshape(1), pair.reshape(2, SLICE, D), *in_hbm(gain.reshape(1, D), *weights, bias.reshape(tiles)))


def attend_kernel(core_ref, block, swapped, gain, wq_h, wq_l, wkv_h, wkv_l, bias, other, out, held, sems):
    core = core_ref[0]
    copies = []
    for g in range(GROUPS):
        heads = pl.ds(g * GROUP, GROUP)
        pair = [
            pltpu.make_async_copy(source, held.at[at, heads], sems.at[g, i])
            for i, (source, at) in enumerate(((bias.at[heads, :, core], core), (other.at[heads], 1 - core)))
        ]
        for copy in pair:
            copy.start()
        copies.append(pair)
    first = core == 0
    own, given = block[...], swapped[...]
    q_rows = jnp.where(first, block[:, pl.ds(core, 1)], swapped[:, pl.ds(core, 1)]).reshape(TOKENS // 2, D)
    k_rows = jnp.where(first, given, own).reshape(TOKENS, D)
    q_norm = split(layer_norm(q_rows, gain[:1]))
    k_norm = split(layer_norm(k_rows, gain[:1]))
    half = TOKENS // 2
    slot = lax.shift_right_logical(iota((half, LANES), 1), 5)
    within = iota((half, LANES), 1) & (SLOT - 1)
    ones = jnp.where((iota((TOKENS, LANES), 1) & (SLOT - 1)) == TOTAL, 1.0, 0.0).astype(F32)
    scale = 1.0 / WIDTH**0.5
    for g in range(GROUPS):
        cols = slice(g * LANES, (g + 1) * LANES)
        query = dot3(q_norm, (wq_h[:, cols], wq_l[:, cols])) * scale
        cols = slice(2 * g * LANES, 2 * (g + 1) * LANES)
        pairs = dot3(k_norm, (wkv_h[:, cols], wkv_l[:, cols]))
        key_h, key_l = split(pairs[:, :LANES])
        value_h, value_l = split(pairs[:, LANES:] + ones)
        query_h, query_l = split(query)
        zero = jnp.zeros_like(query_h)
        lhs_h = jnp.concatenate([jnp.where(slot == p, query_h, zero) for p in range(GROUP)])
        lhs_l = jnp.concatenate([jnp.where(slot == p, query_l, zero) for p in range(GROUP)])
        scores = dot_t(jnp.concatenate((lhs_h, lhs_l), 1), jnp.concatenate((key_h, key_h), 1)) + dot_t(lhs_h, key_l)
        for copy in copies[g]:
            copy.wait()
        tops, parts_h, parts_l = [], [], []
        for p in range(GROUP):
            h = g * GROUP + p
            added = jnp.concatenate([held[k, h].reshape(half, LANES) for k in range(2)], 1)
            one = scores[p * half : (p + 1) * half] + added
            top = jnp.max(one, axis=-1, keepdims=True)
            part_h, part_l = split(jnp.exp(one - top))
            tops.append(top)
            parts_h.append(part_h)
            parts_l.append(part_l)
        sums = dot(jnp.concatenate(parts_h), jnp.concatenate((value_h, value_l), 1))
        sums = sums[:, :LANES] + (sums[:, LANES:] + dot(jnp.concatenate(parts_l), value_h))
        tile = jnp.zeros((half, LANES), F32)
        for p in range(GROUP):
            one = jnp.where(within == TOP, tops[p], sums[p * half : (p + 1) * half])
            tile = jnp.where(slot == p, one, tile)
        out[:, :, g * LANES : (g + 1) * LANES] = tile.reshape(CHIPS, SLICE, LANES)


def attend(core, block, swapped, gain, weights, bias, other):
    vmem, hbm = pl.BlockSpec(memory_space=pltpu.VMEM), pl.BlockSpec(memory_space=pl.ANY)
    shape = (CHIPS, 2, SLICE, D)
    tiles = (HEADS, CHIPS, 2, SLICE, LANES)
    return pl.pallas_call(
        attend_kernel,
        out_shape=jax.ShapeDtypeStruct((CHIPS, SLICE, PAD), F32),
        in_specs=[pl.BlockSpec(memory_space=pltpu.SMEM)] + [vmem] * 7 + [hbm] * 2,
        out_specs=vmem,
        scratch_shapes=[pltpu.VMEM((2, HEADS, CHIPS, SLICE, LANES), F32), pltpu.SemaphoreType.DMA((GROUPS, 2))],
        compiler_params=pltpu.CompilerParams(vmem_limit_bytes=14 << 20),
        cost_estimate=pl.CostEstimate(flops=10**9, bytes_accessed=6 << 20, transcendentals=HEADS * 2**15),
        name="attend",
    )(core.reshape(1), block.reshape(shape), swapped.reshape(shape), gain, *weights, *in_hbm(bias.reshape(tiles), other))


def finish_kernel(parts, gate, wo_h, wo_l, singles, out):
    lane = iota((CHIPS * SLICE, LANES), 1)
    tops_at = lane - (lane & (SLOT - 1)) + TOP
    totals_at = tops_at[:SLICE] - TOP + TOTAL
    gated = []
    for g in range(GROUPS):
        cols = slice(g * LANES, (g + 1) * LANES)
        part = parts[:, :, cols]
        tops = jnp.take_along_axis(part.reshape(CHIPS * SLICE, LANES), tops_at, axis=1).reshape(CHIPS, SLICE, LANES)
        share = jnp.exp(tops - jnp.max(tops, axis=0, keepdims=True))
        sums = jnp.sum(part * share, axis=0)
        totals = jnp.take_along_axis(sums, totals_at, axis=1)
        gated.append(sums / totals * gate[:, cols])
    out[...] = singles[...] + dot3(split(jnp.concatenate(gated, 1)), (wo_h[...], wo_l[...]))


def finish(*args):
    return pl.pallas_call(
        finish_kernel,
        out_shape=jax.ShapeDtypeStruct((SLICE, D), F32),
        compiler_params=pltpu.CompilerParams(vmem_limit_bytes=4 << 20),
        cost_estimate=pl.CostEstimate(flops=6 * SLICE * PAD * D, bytes_accessed=2 << 20, transcendentals=CHIPS * SLICE * PAD),
        name="finish",
    )(*args)


def body(singles, norm_gain, w_query, w_key, w_value, w_gate, w_out, pair_bias):
    core = lax.axis_index("col") % 2
    beside = lax.ppermute(singles, AXES, SIBLING)
    pair = jnp.where(core == 0, jnp.concatenate((singles, beside)), jnp.concatenate((beside, singles)))
    moved = lax.ppermute(pair, AXES, TO_COLUMN)
    *ready, gain, theirs = prepare(core, pair, norm_gain, (w_query, w_key, w_value, w_gate, w_out), pair_bias)
    other = lax.ppermute(theirs, AXES, SIBLING)
    moved, *ready = lax.optimization_barrier((moved, *ready))
    gate = ready[-1]
    piece = jnp.where(core == 0, pair, moved)
    block = exchange(jnp.broadcast_to(piece[None], (CHIPS, 2 * SLICE, D)), MIXED)
    swapped = lax.ppermute(block, AXES, SIBLING)
    message = attend(core, block, swapped, gain, ready[:4], pair_bias, other)
    parts = exchange(message, OVER_M)
    return finish(parts, gate, *ready[4:6], singles)


def solution(mesh):
    return jax.shard_map(
        body,
        mesh=mesh,
        in_specs=(P(("row", "col"), None), P(), P(), P(), P(), P(), P(), P(None, "row", "col")),
        out_specs=P(("row", "col"), None),
        check_vma=False,
    )
```

```python
import jax
import jax.numpy as jnp
from jax import lax
from jax.experimental import pallas as pl
from jax.experimental.pallas import tpu as pltpu
from jax.sharding import PartitionSpec as P

ROW, COL, CHIPS = 16, 32, 16
SLICE = 8
D, HEADS, WIDTH = 384, 16, 24
TOKENS = 256
SLOT = 32
PAD = HEADS * SLOT
GROUP = 4
GROUPS = HEADS // GROUP
LANES = 128
TOTAL, TOP = WIDTH, WIDTH + 1
F32, BF16 = jnp.float32, jnp.bfloat16


def ring(a, b, n):
    return min((a - b) % n, (b - a) % n)


def holders(m):
    z, x_hi = divmod(m, 2)
    x_lo, y = divmod(m, 8)
    zs = sorted(range(8), key=lambda v: (-ring(v, z, 8), v))
    ys = sorted(range(8), key=lambda v: (ring(v, y, 8), v))
    out = [0] * CHIPS
    for z_from, y_to in zip(zs, ys):
        for x_from in range(2):
            out[2 * z_from + x_from] = (x_lo if x_from == x_hi else 1 - x_lo) * 8 + y_to
    return out


HOLDERS = [holders(m) for m in range(CHIPS)]
OVER_M = [[r * COL + 2 * m + k for m in range(CHIPS)] for r in range(ROW) for k in range(2)]
SIBLING = [(i, i ^ 1) for i in range(ROW * COL)]


MIXED = [[r * COL + 2 * m for m in range(CHIPS)] for r in range(ROW)] + [
    [r * COL + 2 * m + 1 for r in HOLDERS[m]] for m in range(CHIPS)
]
TO_COLUMN = [(m * COL + 2 * s, HOLDERS[m][s] * COL + 2 * m + 1) for m in range(CHIPS) for s in range(CHIPS)]


AXES = ("row", "col")


def exchange(pieces, groups):
    return lax.all_to_all(pieces, AXES, 0, 0, tiled=True, axis_index_groups=groups)


def layer_norm(rows):
    mean = jnp.mean(rows, axis=-1, keepdims=True)
    centred = rows - mean
    var = jnp.mean(centred * centred, axis=-1, keepdims=True)
    return centred * lax.rsqrt(var + 1e-05)


def split(array):
    high = array.astype(BF16)
    return high, (array - high.astype(F32)).astype(BF16)


def dot(a, b):
    return lax.dot_general(a, b, (((1,), (0,)), ((), ())), preferred_element_type=F32)


def dot_t(a, b):
    return lax.dot_general(a, b, (((1,), (1,)), ((), ())), preferred_element_type=F32)


def left(high, low):
    return jnp.concatenate((high, low, high), 1)


def right(high, low, dim=1):
    return jnp.concatenate((high, high, low), dim)


def iota(shape, dim):
    return lax.broadcasted_iota(jnp.int32, shape, dim)


def pad_heads(rows, out):
    empty = jnp.zeros((SLOT - WIDTH, D), BF16)
    for h in range(HEADS):
        out[SLOT * h : SLOT * (h + 1), :] = jnp.concatenate((rows[WIDTH * h : WIDTH * (h + 1)], empty))


def fetch(sources, targets, sems):
    copies = [pltpu.make_async_copy(a, b, sems.at[i]) for i, (a, b) in enumerate(zip(sources, targets))]
    for copy in copies:
        copy.start()
    return copies


def prepare_kernel(
    core_ref, pair, gain, w_gate, w_query, w_key, w_value, w_out, bias,
    wt_h, wt_l, wo_h, wo_l, gate, theirs, gain_in, held, gate_h, gate_l, half, sems,
):
    core = core_ref[0]
    weights = (w_gate, w_query, w_key, w_value, w_out)
    copies = fetch((gain, *weights), [gain_in] + [held.at[i] for i in range(5)], sems)
    out = pltpu.make_async_copy(bias.at[:, :, 1 - core], half, sems.at[6])
    out.start()
    copies[0].wait()
    normed = split(layer_norm(pair[:SLICE]) * gain_in[...])
    copies[1].wait()
    high, low = split(held[0].T)
    pad_heads(high, gate_h)
    pad_heads(low, gate_l)
    gate[...] = jax.nn.sigmoid(dot_t(left(*normed), right(gate_h[...], gate_l[...])))
    for i in range(3):
        copies[i + 2].wait()
        at = pl.ds(i * PAD, PAD)
        high, low = split(held[i + 1].T * gain_in[...])
        pad_heads(high, wt_h.at[at])
        pad_heads(low, wt_l.at[at])
        if i == 1:
            out.wait()
            back = pltpu.make_async_copy(half, theirs, sems.at[7])
            back.start()
    copies[5].wait()
    high, low = split(held[4])
    pad_heads(high, wo_h)
    pad_heads(low, wo_l)
    back.wait()


def in_hbm(*arrays):
    return [pltpu.with_memory_space_constraint(array, pltpu.HBM) for array in arrays]


def prepare(core, pair, gain, weights, bias):
    vmem, hbm = pl.BlockSpec(memory_space=pltpu.VMEM), pl.BlockSpec(memory_space=pl.ANY)
    part = (HEADS, CHIPS, SLICE, LANES)
    return pl.pallas_call(
        prepare_kernel,
        out_shape=[pltpu.VMEM(s, BF16) for s in [(3 * PAD, D)] * 2 + [(PAD, D)] * 2]
        + [pltpu.VMEM((SLICE, PAD), F32), pltpu.HBM(part, F32)],
        in_specs=[pl.BlockSpec(memory_space=pltpu.SMEM)] + [vmem] + [hbm] * 7,
        out_specs=[vmem] * 5 + [hbm],
        scratch_shapes=[pltpu.VMEM((1, D), F32), pltpu.VMEM((5, D, D), F32)]
        + [pltpu.VMEM((PAD, D), BF16)] * 2
        + [pltpu.VMEM(part, F32), pltpu.SemaphoreType.DMA((8,))],
        compiler_params=pltpu.CompilerParams(vmem_limit_bytes=20 << 20),
        cost_estimate=pl.CostEstimate(flops=2 * 2304 * D * PAD, bytes_accessed=8 << 20, transcendentals=SLICE * D),
        name="prepare",
    )(core.reshape(1), pair, *in_hbm(gain.reshape(1, D), *weights, bias.reshape(HEADS, CHIPS, 2, SLICE, LANES)))


def attend_kernel(core_ref, block, swapped, wt_h, wt_l, bias, other, out, held, sems):
    core = core_ref[0]
    copies = []
    for g in range(GROUPS):
        heads = pl.ds(g * GROUP, GROUP)
        pair = [
            pltpu.make_async_copy(source, held.at[at, heads], sems.at[g, i])
            for i, (source, at) in enumerate(((bias.at[heads, :, core], core), (other.at[heads], 1 - core)))
        ]
        for copy in pair:
            copy.start()
        copies.append(pair)
    first = core == 0
    own, given = block[...], swapped[...]
    q_rows = jnp.where(first, block[:, pl.ds(core, 1)], swapped[:, pl.ds(core, 1)]).reshape(TOKENS // 2, D)
    k_rows = jnp.where(first, given, own).reshape(TOKENS, D)
    q_norm = right(*split(layer_norm(q_rows)))
    k_norm = right(*split(layer_norm(k_rows)))
    half = TOKENS // 2
    queries = dot_t(left(wt_h[:PAD], wt_l[:PAD]), q_norm) * (1.0 / WIDTH**0.5)
    pairs = dot_t(left(wt_h[PAD:], wt_l[PAD:]), k_norm)
    slot = lax.shift_right_logical(iota((half, LANES), 1), 5)
    within = iota((half, LANES), 1) & (SLOT - 1)
    ones = jnp.where((iota((LANES, TOKENS), 0) & (SLOT - 1)) == TOTAL, 1.0, 0.0).astype(F32)
    for g in range(GROUPS):
        at = g * LANES
        query_h, query_l = split(queries[at : at + LANES].T)
        key = right(*split(pairs[at : at + LANES]), 0)
        value_h, value_l = split(pairs[PAD + at : PAD + at + LANES] + ones)
        zero = jnp.zeros_like(query_h)
        lhs_h = jnp.concatenate([jnp.where(slot == p, query_h, zero) for p in range(GROUP)])
        lhs_l = jnp.concatenate([jnp.where(slot == p, query_l, zero) for p in range(GROUP)])
        scores = dot(left(lhs_h, lhs_l), key)
        for copy in copies[g]:
            copy.wait()
        tops, parts_h, parts_l = [], [], []
        for p in range(GROUP):
            h = g * GROUP + p
            added = jnp.concatenate([held[k, h].reshape(half, LANES) for k in range(2)], 1)
            one = scores[p * half : (p + 1) * half] + added
            top = jnp.max(one, axis=-1, keepdims=True)
            part_h, part_l = split(jnp.exp(one - top))
            tops.append(top)
            parts_h.append(part_h)
            parts_l.append(part_l)
        sums = dot_t(jnp.concatenate(parts_h), jnp.concatenate((value_h, value_l)))
        sums = sums[:, :LANES] + (sums[:, LANES:] + dot_t(jnp.concatenate(parts_l), value_h))
        tile = jnp.zeros((half, LANES), F32)
        for p in range(GROUP):
            one = jnp.where(within == TOP, tops[p], sums[p * half : (p + 1) * half])
            tile = jnp.where(slot == p, one, tile)
        out[:, :, g * LANES : (g + 1) * LANES] = tile.reshape(CHIPS, SLICE, LANES)


def attend(core, block, swapped, weights, bias, other):
    vmem, hbm = pl.BlockSpec(memory_space=pltpu.VMEM), pl.BlockSpec(memory_space=pl.ANY)
    shape = (CHIPS, 2, SLICE, D)
    tiles = (HEADS, CHIPS, 2, SLICE, LANES)
    return pl.pallas_call(
        attend_kernel,
        out_shape=jax.ShapeDtypeStruct((CHIPS, SLICE, PAD), F32),
        in_specs=[pl.BlockSpec(memory_space=pltpu.SMEM)] + [vmem] * 4 + [hbm] * 2,
        out_specs=vmem,
        scratch_shapes=[pltpu.VMEM((2, HEADS, CHIPS, SLICE, LANES), F32), pltpu.SemaphoreType.DMA((GROUPS, 2))],
        compiler_params=pltpu.CompilerParams(vmem_limit_bytes=20 << 20),
        cost_estimate=pl.CostEstimate(flops=10**9, bytes_accessed=6 << 20, transcendentals=HEADS * 2**15),
        name="attend",
    )(core.reshape(1), block.reshape(shape), swapped.reshape(shape), *weights, *in_hbm(bias.reshape(tiles)), other)


def finish_kernel(parts, gate, wo_h, wo_l, singles, out):
    lane = iota((CHIPS * SLICE, LANES), 1)
    tops_at = lane - (lane & (SLOT - 1)) + TOP
    totals_at = tops_at[:SLICE] - TOP + TOTAL
    gated = []
    for g in range(GROUPS):
        cols = slice(g * LANES, (g + 1) * LANES)
        part = parts[:, :, cols]
        tops = jnp.take_along_axis(part.reshape(CHIPS * SLICE, LANES), tops_at, axis=1).reshape(CHIPS, SLICE, LANES)
        share = jnp.exp(tops - jnp.max(tops, axis=0, keepdims=True))
        sums = jnp.sum(part * share, axis=0)
        totals = jnp.take_along_axis(sums, totals_at, axis=1)
        gated.append(sums / totals * gate[:, cols])
    out[...] = singles[...] + dot(left(*split(jnp.concatenate(gated, 1))), right(wo_h[...], wo_l[...], 0))


def finish(*args):
    return pl.pallas_call(
        finish_kernel,
        out_shape=jax.ShapeDtypeStruct((SLICE, D), F32),
        compiler_params=pltpu.CompilerParams(vmem_limit_bytes=4 << 20),
        cost_estimate=pl.CostEstimate(flops=6 * SLICE * PAD * D, bytes_accessed=2 << 20, transcendentals=CHIPS * SLICE * PAD),
        name="finish",
    )(*args)


def body(singles, norm_gain, w_query, w_key, w_value, w_gate, w_out, pair_bias):
    core = lax.axis_index("col") % 2
    beside = lax.ppermute(singles, AXES, SIBLING)
    pair = jnp.concatenate((singles, beside))
    moved = lax.ppermute(pair, AXES, TO_COLUMN)
    *ready, theirs = prepare(core, pair, norm_gain, (w_gate, w_query, w_key, w_value, w_out), pair_bias)
    other = lax.ppermute(theirs, AXES, SIBLING)
    moved, *ready = lax.optimization_barrier((moved, *ready))
    wt_h, wt_l, wo_h, wo_l, gate = ready
    piece = jnp.where(core == 0, pair, moved)
    block = exchange(jnp.broadcast_to(piece[None], (CHIPS, 2 * SLICE, D)), MIXED)
    swapped = lax.ppermute(block, AXES, SIBLING)
    message = attend(core, block, swapped, (wt_h, wt_l), pair_bias, other)
    parts = exchange(message, OVER_M)
    return finish(parts, gate, wo_h, wo_l, singles)


def solution(mesh):
    return jax.shard_map(
        body,
        mesh=mesh,
        in_specs=(P(("row", "col"), None), P(), P(), P(), P(), P(), P(), P(None, "row", "col")),
        out_specs=P(("row", "col"), None),
        check_vma=False,
    )
```

```python
import jax
import jax.numpy as jnp
from jax import lax
from jax.experimental import pallas as pl
from jax.experimental.pallas import tpu as pltpu
from jax.sharding import PartitionSpec as P

ROW, COL, CHIPS = 16, 32, 16
SLICE = 8
D, HEADS, WIDTH = 384, 16, 24
TOKENS = 256
SLOT = 32
PAD = HEADS * SLOT
GROUP = 4
GROUPS = HEADS // GROUP
LANES = 128
TOTAL, TOP = WIDTH, WIDTH + 1
F32, BF16 = jnp.float32, jnp.bfloat16


def ring(a, b, n):
    return min((a - b) % n, (b - a) % n)


def holders(m):
    z, x_hi = divmod(m, 2)
    x_lo, y = divmod(m, 8)
    zs = sorted(range(8), key=lambda v: (-ring(v, z, 8), v))
    ys = sorted(range(8), key=lambda v: (ring(v, y, 8), v))
    out = [0] * CHIPS
    for z_from, y_to in zip(zs, ys):
        for x_from in range(2):
            out[2 * z_from + x_from] = (x_lo if x_from == x_hi else 1 - x_lo) * 8 + y_to
    return out


HOLDERS = [holders(m) for m in range(CHIPS)]
OVER_M = [[r * COL + 2 * m + k for m in range(CHIPS)] for r in range(ROW) for k in range(2)]
SIBLING = [(i, i ^ 1) for i in range(ROW * COL)]


MIXED = [[r * COL + 2 * m for m in range(CHIPS)] for r in range(ROW)] + [
    [r * COL + 2 * m + 1 for r in HOLDERS[m]] for m in range(CHIPS)
]
TO_COLUMN = [(m * COL + 2 * s, HOLDERS[m][s] * COL + 2 * m + 1) for m in range(CHIPS) for s in range(CHIPS)]


AXES = ("row", "col")


def exchange(pieces, groups):
    return lax.all_to_all(pieces, AXES, 0, 0, tiled=True, axis_index_groups=groups)


def layer_norm(rows):
    mean = jnp.mean(rows, axis=-1, keepdims=True)
    centred = rows - mean
    var = jnp.mean(centred * centred, axis=-1, keepdims=True)
    return centred * lax.rsqrt(var + 1e-05)


def split(array):
    high = array.astype(BF16)
    return high, (array - high.astype(F32)).astype(BF16)


def dot(a, b):
    return lax.dot_general(a, b, (((1,), (0,)), ((), ())), preferred_element_type=F32)


def dot_t(a, b):
    return lax.dot_general(a, b, (((1,), (1,)), ((), ())), preferred_element_type=F32)


def left(high, low):
    return jnp.concatenate((high, low, high), 1)


def right(high, low, dim=1):
    return jnp.concatenate((high, high, low), dim)


def iota(shape, dim):
    return lax.broadcasted_iota(jnp.int32, shape, dim)


def pad_heads(rows, out):
    empty = jnp.zeros((SLOT - WIDTH, D), BF16)
    for h in range(HEADS):
        out[SLOT * h : SLOT * (h + 1), :] = jnp.concatenate((rows[WIDTH * h : WIDTH * (h + 1)], empty))


def fetch(sources, targets, sems):
    copies = [pltpu.make_async_copy(a, b, sems.at[i]) for i, (a, b) in enumerate(zip(sources, targets))]
    for copy in copies:
        copy.start()
    return copies


def prepare_kernel(
    core_ref, pair, gain, w_out, w_gate, w_query, w_key, w_value, bias,
    wt_h, wt_l, wo_h, wo_l, gate, theirs, gain_in, held, gate_h, gate_l, out_h, out_l, half, sems,
):
    core = core_ref[0]
    weights = (w_out, w_gate, w_query, w_key, w_value)
    copies = fetch((gain, *weights), [gain_in.at[0]] + [held.at[i] for i in range(5)], sems)
    out = pltpu.make_async_copy(bias.at[:, :, 1 - core], half, sems.at[6])
    out.start()
    copies[0].wait()
    normed = split(layer_norm(pair[:SLICE]) * gain_in[...])
    copies[1].wait()
    high, low = split(held[0])
    pad_heads(high, out_h)
    pad_heads(low, out_l)
    backs = fetch((out_h, out_l), (wo_h, wo_l), sems.at[pl.ds(8, 2)])
    copies[2].wait()
    high, low = split(held[1].T)
    pad_heads(high, gate_h)
    pad_heads(low, gate_l)
    gate[...] = jax.nn.sigmoid(dot_t(left(*normed), right(gate_h[...], gate_l[...])))
    for i in range(3):
        copies[i + 3].wait()
        at = pl.ds(i * D, D)
        wt_h[at], wt_l[at] = split(held[i + 2].T * gain_in[...])
        if i == 1:
            out.wait()
            back = pltpu.make_async_copy(half, theirs, sems.at[7])
            back.start()
    for copy in (back, *backs):
        copy.wait()


def in_hbm(*arrays):
    return [pltpu.with_memory_space_constraint(array, pltpu.HBM) for array in arrays]


def prepare(core, pair, gain, weights, bias):
    vmem, hbm = pl.BlockSpec(memory_space=pltpu.VMEM), pl.BlockSpec(memory_space=pl.ANY)
    part = (HEADS, CHIPS, SLICE, LANES)
    return pl.pallas_call(
        prepare_kernel,
        out_shape=[pltpu.VMEM((3 * D, D), BF16)] * 2
        + [pltpu.HBM((PAD, D), BF16)] * 2
        + [pltpu.VMEM((SLICE, PAD), F32), pltpu.HBM(part, F32)],
        in_specs=[pl.BlockSpec(memory_space=pltpu.SMEM)] + [vmem] + [hbm] * 7,
        out_specs=[vmem] * 2 + [hbm] * 2 + [vmem, hbm],
        scratch_shapes=[pltpu.VMEM((1, D), F32), pltpu.VMEM((5, D, D), F32)]
        + [pltpu.VMEM((PAD, D), BF16)] * 4
        + [pltpu.VMEM(part, F32), pltpu.SemaphoreType.DMA((10,))],
        compiler_params=pltpu.CompilerParams(vmem_limit_bytes=20 << 20),
        cost_estimate=pl.CostEstimate(flops=2 * 2304 * D * PAD, bytes_accessed=8 << 20, transcendentals=SLICE * D),
        name="prepare",
    )(core.reshape(1), pair, *in_hbm(gain, *weights, bias.reshape(HEADS, CHIPS, 2, SLICE, LANES)))


def stage_kernel(core_ref, bias, other, held, sems):
    core = core_ref[0]
    for copy in fetch((bias.at[:, :, core], other), (held.at[core], held.at[1 - core]), sems):
        copy.wait()


def stage(core, bias, other):
    hbm = pl.BlockSpec(memory_space=pl.ANY)
    return pl.pallas_call(
        stage_kernel,
        out_shape=pltpu.VMEM((2, HEADS, CHIPS, SLICE, LANES), F32),
        in_specs=[pl.BlockSpec(memory_space=pltpu.SMEM)] + [hbm] * 2,
        out_specs=pl.BlockSpec(memory_space=pltpu.VMEM),
        scratch_shapes=[pltpu.SemaphoreType.DMA((2,))],
        compiler_params=pltpu.CompilerParams(vmem_limit_bytes=20 << 20),
        cost_estimate=pl.CostEstimate(flops=0, bytes_accessed=4 << 20, transcendentals=0),
        name="stage",
    )(core.reshape(1), *in_hbm(bias.reshape(HEADS, CHIPS, 2, SLICE, LANES)), other)


def attend_kernel(core_ref, block, swapped, wt_h, wt_l, held, out):
    core = core_ref[0]
    first = core == 0
    own, given = block[...], swapped[...]
    q_rows = jnp.where(first, block[:, pl.ds(core, 1)], swapped[:, pl.ds(core, 1)]).reshape(TOKENS // 2, D)
    k_rows = jnp.where(first, given, own).reshape(TOKENS, D)
    q_norm = right(*split(layer_norm(q_rows)))
    k_norm = right(*split(layer_norm(k_rows)))
    half = TOKENS // 2
    queries = dot_t(left(wt_h[:D], wt_l[:D]), q_norm) * (1.0 / WIDTH**0.5)
    pairs = dot_t(left(wt_h[D:], wt_l[D:]), k_norm)
    slot = lax.shift_right_logical(iota((half, LANES), 1), 5)
    within = iota((half, LANES), 1) & (SLOT - 1)
    blank = jnp.zeros((SLOT - WIDTH, half), F32)
    blank_key = jnp.zeros((SLOT - WIDTH, TOKENS), F32)
    ones = jnp.where(iota((SLOT - WIDTH, TOKENS), 0) == TOTAL - WIDTH, 1.0, 0.0).astype(F32)

    def slots(rows, first, filler):
        parts = []
        for p in range(GROUP):
            parts += [rows[first + p * WIDTH : first + (p + 1) * WIDTH], filler]
        return jnp.concatenate(parts)

    for g in range(GROUPS):
        at = g * GROUP * WIDTH
        query_h, query_l = split(slots(queries, at, blank).T)
        key = right(*split(slots(pairs, at, blank_key)), 0)
        value_h, value_l = split(slots(pairs, D + at, ones))
        zero = jnp.zeros_like(query_h)
        lhs_h = jnp.concatenate([jnp.where(slot == p, query_h, zero) for p in range(GROUP)])
        lhs_l = jnp.concatenate([jnp.where(slot == p, query_l, zero) for p in range(GROUP)])
        scores = dot(left(lhs_h, lhs_l), key)
        tops, parts_h, parts_l = [], [], []
        for p in range(GROUP):
            h = g * GROUP + p
            added = jnp.concatenate([held[k, h].reshape(half, LANES) for k in range(2)], 1)
            one = scores[p * half : (p + 1) * half] + added
            top = jnp.max(one, axis=-1, keepdims=True)
            part_h, part_l = split(jnp.exp(one - top))
            tops.append(top)
            parts_h.append(part_h)
            parts_l.append(part_l)
        sums = dot_t(jnp.concatenate(parts_h), jnp.concatenate((value_h, value_l)))
        sums = sums[:, :LANES] + (sums[:, LANES:] + dot_t(jnp.concatenate(parts_l), value_h))
        tile = jnp.zeros((half, LANES), F32)
        for p in range(GROUP):
            one = jnp.where(within == TOP, tops[p], sums[p * half : (p + 1) * half])
            tile = jnp.where(slot == p, one, tile)
        out[:, :, g * LANES : (g + 1) * LANES] = tile.reshape(CHIPS, SLICE, LANES)


def attend(core, block, swapped, weights, staged):
    vmem = pl.BlockSpec(memory_space=pltpu.VMEM)
    shape = (CHIPS, 2, SLICE, D)
    return pl.pallas_call(
        attend_kernel,
        out_shape=jax.ShapeDtypeStruct((CHIPS, SLICE, PAD), F32),
        in_specs=[pl.BlockSpec(memory_space=pltpu.SMEM)] + [vmem] * 5,
        out_specs=vmem,
        compiler_params=pltpu.CompilerParams(vmem_limit_bytes=20 << 20),
        cost_estimate=pl.CostEstimate(flops=10**9, bytes_accessed=6 << 20, transcendentals=HEADS * 2**15),
        name="attend",
    )(core.reshape(1), block.reshape(shape), swapped.reshape(shape), *weights, staged)


def finish_kernel(parts, gate, wo_h, wo_l, singles, out):
    lane = iota((CHIPS * SLICE, LANES), 1)
    tops_at = lane - (lane & (SLOT - 1)) + TOP
    totals_at = tops_at[:SLICE] - TOP + TOTAL
    gated = []
    for g in range(GROUPS):
        cols = slice(g * LANES, (g + 1) * LANES)
        part = parts[:, :, cols]
        tops = jnp.take_along_axis(part.reshape(CHIPS * SLICE, LANES), tops_at, axis=1).reshape(CHIPS, SLICE, LANES)
        share = jnp.exp(tops - jnp.max(tops, axis=0, keepdims=True))
        sums = jnp.sum(part * share, axis=0)
        totals = jnp.take_along_axis(sums, totals_at, axis=1)
        gated.append(sums / totals * gate[:, cols])
    high, low = split(jnp.concatenate(gated, 1))
    both = dot(jnp.concatenate((high, low)), wo_h[...])
    out[...] = singles[...] + (both[:SLICE] + (both[SLICE:] + dot(high, wo_l[...])))


def finish(*args):
    return pl.pallas_call(
        finish_kernel,
        out_shape=jax.ShapeDtypeStruct((SLICE, D), F32),
        compiler_params=pltpu.CompilerParams(vmem_limit_bytes=4 << 20),
        cost_estimate=pl.CostEstimate(flops=6 * SLICE * PAD * D, bytes_accessed=2 << 20, transcendentals=CHIPS * SLICE * PAD),
        name="finish",
    )(*args)


def body(singles, norm_gain, w_query, w_key, w_value, w_gate, w_out, pair_bias):
    core = lax.axis_index("col") % 2
    beside = lax.ppermute(singles, AXES, SIBLING)
    pair = jnp.concatenate((singles, beside))
    moved = lax.ppermute(pair, AXES, TO_COLUMN)
    wt_h, wt_l, wo_h, wo_l, gate, theirs = prepare(core, pair, norm_gain, (w_out, w_gate, w_query, w_key, w_value), pair_bias)
    other = lax.ppermute(theirs, AXES, SIBLING)
    moved, wt_h, wt_l, gate = lax.optimization_barrier((moved, wt_h, wt_l, gate))
    piece = jnp.where(core == 0, pair, moved)
    block = exchange(jnp.broadcast_to(piece[None], (CHIPS, 2 * SLICE, D)), MIXED)
    swapped = lax.ppermute(block, AXES, SIBLING)
    message = attend(core, block, swapped, (wt_h, wt_l), stage(core, pair_bias, other))
    parts = exchange(message, OVER_M)
    return finish(parts, gate, wo_h, wo_l, singles)


def solution(mesh):
    return jax.shard_map(
        body,
        mesh=mesh,
        in_specs=(P(("row", "col"), None), P(), P(), P(), P(), P(), P(), P(None, "row", "col")),
        out_specs=P(("row", "col"), None),
        check_vma=False,
    )
```

```python
import jax
import jax.numpy as jnp
from jax import lax
from jax.experimental import pallas as pl
from jax.experimental.pallas import tpu as pltpu
from jax.sharding import PartitionSpec as P

ROW, COL, CHIPS = 16, 32, 16
SLICE = 8
D, HEADS, WIDTH = 384, 16, 24
TOKENS = 256
SLOT = 32
PAD = HEADS * SLOT
GROUP = 4
GROUPS = HEADS // GROUP
LANES = 128
TOTAL, TOP = WIDTH, WIDTH + 1
F32, BF16 = jnp.float32, jnp.bfloat16


def ring(a, b, n):
    return min((a - b) % n, (b - a) % n)


def holders(m):
    z, x_hi = divmod(m, 2)
    x_lo, y = divmod(m, 8)
    zs = sorted(range(8), key=lambda v: (-ring(v, z, 8), v))
    ys = sorted(range(8), key=lambda v: (ring(v, y, 8), v))
    out = [0] * CHIPS
    for z_from, y_to in zip(zs, ys):
        for x_from in range(2):
            out[2 * z_from + x_from] = (x_lo if x_from == x_hi else 1 - x_lo) * 8 + y_to
    return out


HOLDERS = [holders(m) for m in range(CHIPS)]
OVER_M = [[r * COL + 2 * m + k for m in range(CHIPS)] for r in range(ROW) for k in range(2)]
SIBLING = [(i, i ^ 1) for i in range(ROW * COL)]


MIXED = [[r * COL + 2 * m for m in range(CHIPS)] for r in range(ROW)] + [
    [r * COL + 2 * m + 1 for r in HOLDERS[m]] for m in range(CHIPS)
]


def to_column(core):
    return [(m * COL + 2 * s + core, HOLDERS[m][s] * COL + 2 * m + 1) for m in range(CHIPS) for s in range(CHIPS)]


TO_COLUMN_1 = to_column(1)
TO_COLUMN_0 = to_column(0) + [(i, i - 1) for i in range(1, ROW * COL, 2)]


AXES = ("row", "col")


def exchange(pieces, groups):
    return lax.all_to_all(pieces, AXES, 0, 0, tiled=True, axis_index_groups=groups)


def layer_norm(rows):
    mean = jnp.mean(rows, axis=-1, keepdims=True)
    centred = rows - mean
    var = jnp.mean(centred * centred, axis=-1, keepdims=True)
    return centred * lax.rsqrt(var + 1e-05)


def split(array):
    high = array.astype(BF16)
    return high, (array - high.astype(F32)).astype(BF16)


def dot(a, b):
    return lax.dot_general(a, b, (((1,), (0,)), ((), ())), preferred_element_type=F32)


def dot_t(a, b):
    return lax.dot_general(a, b, (((1,), (1,)), ((), ())), preferred_element_type=F32)


def left(high, low):
    return jnp.concatenate((high, low, high), 1)


def right(high, low, dim=1):
    return jnp.concatenate((high, high, low), dim)


def iota(shape, dim):
    return lax.broadcasted_iota(jnp.int32, shape, dim)


def pad_heads(rows, out):
    empty = jnp.zeros((SLOT - WIDTH, D), BF16)
    for h in range(HEADS):
        out[SLOT * h : SLOT * (h + 1), :] = jnp.concatenate((rows[WIDTH * h : WIDTH * (h + 1)], empty))


def fetch(sources, targets, sems):
    copies = [pltpu.make_async_copy(a, b, sems.at[i]) for i, (a, b) in enumerate(zip(sources, targets))]
    for copy in copies:
        copy.start()
    return copies


def prepare_kernel(
    singles, gain, w_out, w_gate, w_query, w_key, w_value,
    wt_h, wt_l, wo_h, wo_l, gate, singles_in, gain_in, held, gate_h, gate_l, out_h, out_l, sems,
):
    weights = (w_out, w_gate, w_query, w_key, w_value)
    copies = fetch((gain, *weights, singles), [gain_in.at[0]] + [held.at[i] for i in range(5)] + [singles_in], sems)
    copies[0].wait()
    copies[6].wait()
    normed = split(layer_norm(singles_in[...]) * gain_in[...])
    copies[1].wait()
    high, low = split(held[0])
    pad_heads(high, out_h)
    pad_heads(low, out_l)
    backs = fetch((out_h, out_l), (wo_h, wo_l), sems.at[pl.ds(8, 2)])
    copies[2].wait()
    high, low = split(held[1].T)
    pad_heads(high, gate_h)
    pad_heads(low, gate_l)
    gate[...] = jax.nn.sigmoid(dot_t(left(*normed), right(gate_h[...], gate_l[...])))
    for i in range(3):
        copies[i + 3].wait()
        at = pl.ds(i * D, D)
        wt_h[at], wt_l[at] = split(held[i + 2].T * gain_in[...])
    for copy in backs:
        copy.wait()


def in_hbm(*arrays):
    return [pltpu.with_memory_space_constraint(array, pltpu.HBM) for array in arrays]


def prepare(singles, gain, *weights):
    vmem, hbm = pl.BlockSpec(memory_space=pltpu.VMEM), pl.BlockSpec(memory_space=pl.ANY)
    return pl.pallas_call(
        prepare_kernel,
        out_shape=[pltpu.VMEM((3 * D, D), BF16)] * 2 + [pltpu.HBM((PAD, D), BF16)] * 2 + [pltpu.VMEM((SLICE, PAD), F32)],
        in_specs=[hbm] * 7,
        out_specs=[vmem] * 2 + [hbm] * 2 + [vmem],
        scratch_shapes=[pltpu.VMEM((SLICE, D), F32), pltpu.VMEM((1, D), F32), pltpu.VMEM((5, D, D), F32)]
        + [pltpu.VMEM((PAD, D), BF16)] * 4
        + [pltpu.SemaphoreType.DMA((10,))],
        compiler_params=pltpu.CompilerParams(vmem_limit_bytes=20 << 20),
        cost_estimate=pl.CostEstimate(flops=2 * 2304 * D * PAD, bytes_accessed=8 << 20, transcendentals=SLICE * D),
        name="prepare",
    )(*in_hbm(singles, gain, *weights))


def cut_kernel(core_ref, bias, theirs, half, sems):
    for copy in fetch((bias.at[:, :, 1 - core_ref[0]],), (half,), sems):
        copy.wait()
    for copy in fetch((half,), (theirs,), sems.at[pl.ds(1, 1)]):
        copy.wait()


def cut(core, bias):
    part = (HEADS, CHIPS, SLICE, LANES)
    hbm = pl.BlockSpec(memory_space=pl.ANY)
    return pl.pallas_call(
        cut_kernel,
        out_shape=pltpu.HBM(part, F32),
        in_specs=[pl.BlockSpec(memory_space=pltpu.SMEM), hbm],
        out_specs=hbm,
        scratch_shapes=[pltpu.VMEM(part, F32), pltpu.SemaphoreType.DMA((2,))],
        compiler_params=pltpu.CompilerParams(vmem_limit_bytes=20 << 20),
        cost_estimate=pl.CostEstimate(flops=0, bytes_accessed=4 << 20, transcendentals=0),
        name="cut",
    )(core.reshape(1), *in_hbm(bias.reshape(HEADS, CHIPS, 2, SLICE, LANES)))


def stage_kernel(core_ref, bias, other, held, sems):
    core = core_ref[0]
    for copy in fetch((bias.at[:, :, core], other), (held.at[core], held.at[1 - core]), sems):
        copy.wait()


def stage(core, bias, other):
    hbm = pl.BlockSpec(memory_space=pl.ANY)
    return pl.pallas_call(
        stage_kernel,
        out_shape=pltpu.VMEM((2, HEADS, CHIPS, SLICE, LANES), F32),
        in_specs=[pl.BlockSpec(memory_space=pltpu.SMEM)] + [hbm] * 2,
        out_specs=pl.BlockSpec(memory_space=pltpu.VMEM),
        scratch_shapes=[pltpu.SemaphoreType.DMA((2,))],
        compiler_params=pltpu.CompilerParams(vmem_limit_bytes=20 << 20),
        cost_estimate=pl.CostEstimate(flops=0, bytes_accessed=4 << 20, transcendentals=0),
        name="stage",
    )(core.reshape(1), *in_hbm(bias.reshape(HEADS, CHIPS, 2, SLICE, LANES)), other)


def attend_kernel(core_ref, block, swapped, wt_h, wt_l, held, out):
    core = core_ref[0]
    first = core == 0
    own, given = block[...], swapped[...]
    q_rows = jnp.where(first, block[:, pl.ds(core, 1)], swapped[:, pl.ds(core, 1)]).reshape(TOKENS // 2, D)
    k_rows = jnp.where(first, given, own).reshape(TOKENS, D)
    q_norm = right(*split(layer_norm(q_rows)))
    k_norm = right(*split(layer_norm(k_rows)))
    half = TOKENS // 2
    queries = dot_t(left(wt_h[:D], wt_l[:D]), q_norm) * (1.0 / WIDTH**0.5)
    pairs = dot_t(left(wt_h[D:], wt_l[D:]), k_norm)
    slot = lax.shift_right_logical(iota((half, LANES), 1), 5)
    within = iota((half, LANES), 1) & (SLOT - 1)
    blank = jnp.zeros((SLOT - WIDTH, half), F32)
    blank_key = jnp.zeros((SLOT - WIDTH, TOKENS), F32)
    ones = jnp.where(iota((SLOT - WIDTH, TOKENS), 0) == TOTAL - WIDTH, 1.0, 0.0).astype(F32)

    def slots(rows, first, filler):
        parts = []
        for p in range(GROUP):
            parts += [rows[first + p * WIDTH : first + (p + 1) * WIDTH], filler]
        return jnp.concatenate(parts)

    for g in range(GROUPS):
        at = g * GROUP * WIDTH
        query_h, query_l = split(slots(queries, at, blank).T)
        key = right(*split(slots(pairs, at, blank_key)), 0)
        value_h, value_l = split(slots(pairs, D + at, ones))
        zero = jnp.zeros_like(query_h)
        lhs_h = jnp.concatenate([jnp.where(slot == p, query_h, zero) for p in range(GROUP)])
        lhs_l = jnp.concatenate([jnp.where(slot == p, query_l, zero) for p in range(GROUP)])
        scores = dot(left(lhs_h, lhs_l), key)
        tops, parts_h, parts_l = [], [], []
        for p in range(GROUP):
            h = g * GROUP + p
            added = jnp.concatenate([held[k, h].reshape(half, LANES) for k in range(2)], 1)
            one = scores[p * half : (p + 1) * half] + added
            top = jnp.max(one, axis=-1, keepdims=True)
            part_h, part_l = split(jnp.exp(one - top))
            tops.append(top)
            parts_h.append(part_h)
            parts_l.append(part_l)
        sums = dot_t(jnp.concatenate(parts_h), jnp.concatenate((value_h, value_l)))
        sums = sums[:, :LANES] + (sums[:, LANES:] + dot_t(jnp.concatenate(parts_l), value_h))
        tile = jnp.zeros((half, LANES), F32)
        for p in range(GROUP):
            one = jnp.where(within == TOP, tops[p], sums[p * half : (p + 1) * half])
            tile = jnp.where(slot == p, one, tile)
        out[:, :, g * LANES : (g + 1) * LANES] = tile.reshape(CHIPS, SLICE, LANES)


def attend(core, block, swapped, weights, staged):
    vmem = pl.BlockSpec(memory_space=pltpu.VMEM)
    shape = (CHIPS, 2, SLICE, D)
    return pl.pallas_call(
        attend_kernel,
        out_shape=jax.ShapeDtypeStruct((CHIPS, SLICE, PAD), F32),
        in_specs=[pl.BlockSpec(memory_space=pltpu.SMEM)] + [vmem] * 5,
        out_specs=vmem,
        compiler_params=pltpu.CompilerParams(vmem_limit_bytes=20 << 20),
        cost_estimate=pl.CostEstimate(flops=10**9, bytes_accessed=6 << 20, transcendentals=HEADS * 2**15),
        name="attend",
    )(core.reshape(1), block.reshape(shape), swapped.reshape(shape), *weights, staged)


def finish_kernel(parts, gate, wo_h, wo_l, singles, out):
    lane = iota((CHIPS * SLICE, LANES), 1)
    tops_at = lane - (lane & (SLOT - 1)) + TOP
    totals_at = tops_at[:SLICE] - TOP + TOTAL
    gated = []
    for g in range(GROUPS):
        cols = slice(g * LANES, (g + 1) * LANES)
        part = parts[:, :, cols]
        tops = jnp.take_along_axis(part.reshape(CHIPS * SLICE, LANES), tops_at, axis=1).reshape(CHIPS, SLICE, LANES)
        share = jnp.exp(tops - jnp.max(tops, axis=0, keepdims=True))
        sums = jnp.sum(part * share, axis=0)
        totals = jnp.take_along_axis(sums, totals_at, axis=1)
        gated.append(sums / totals * gate[:, cols])
    high, low = split(jnp.concatenate(gated, 1))
    both = dot(jnp.concatenate((high, low)), wo_h[...])
    out[...] = singles[...] + (both[:SLICE] + (both[SLICE:] + dot(high, wo_l[...])))


def finish(*args):
    return pl.pallas_call(
        finish_kernel,
        out_shape=jax.ShapeDtypeStruct((SLICE, D), F32),
        compiler_params=pltpu.CompilerParams(vmem_limit_bytes=4 << 20),
        cost_estimate=pl.CostEstimate(flops=6 * SLICE * PAD * D, bytes_accessed=2 << 20, transcendentals=CHIPS * SLICE * PAD),
        name="finish",
    )(*args)


def body(singles, norm_gain, w_query, w_key, w_value, w_gate, w_out, pair_bias):
    core = lax.axis_index("col") % 2
    moved = lax.ppermute(singles, AXES, TO_COLUMN_1)
    first = lax.ppermute(singles, AXES, TO_COLUMN_0)
    theirs = cut(core, pair_bias)
    moved, first, theirs = lax.optimization_barrier((moved, first, theirs))
    other = lax.ppermute(theirs, AXES, SIBLING)
    piece = jnp.where(core == 0, jnp.concatenate((singles, first)), jnp.concatenate((first, moved)))
    pieces, held = lax.optimization_barrier((jnp.broadcast_to(piece[None], (CHIPS, 2 * SLICE, D)), singles))
    wt_h, wt_l, wo_h, wo_l, gate = prepare(held, norm_gain, w_out, w_gate, w_query, w_key, w_value)
    block = exchange(pieces, MIXED)
    block, wt_h, wt_l, gate = lax.optimization_barrier((block, wt_h, wt_l, gate))
    swapped = lax.ppermute(block, AXES, SIBLING)
    message = attend(core, block, swapped, (wt_h, wt_l), stage(core, pair_bias, other))
    parts = exchange(message, OVER_M)
    return finish(parts, gate, wo_h, wo_l, singles)


def solution(mesh):
    return jax.shard_map(
        body,
        mesh=mesh,
        in_specs=(P(("row", "col"), None), P(), P(), P(), P(), P(), P(), P(None, "row", "col")),
        out_specs=P(("row", "col"), None),
        check_vma=False,
    )
```

```python
import jax
import jax.numpy as jnp
from jax import lax
from jax.experimental import pallas as pl
from jax.experimental.pallas import tpu as pltpu
from jax.sharding import PartitionSpec as P

ROW, COL, CHIPS = 16, 32, 16
SLICE = 8
D, HEADS, WIDTH = 384, 16, 24
TOKENS = 256
SLOT = 32
PAD = HEADS * SLOT
GROUP = 4
GROUPS = HEADS // GROUP
LANES = 128
TOTAL, TOP = WIDTH, WIDTH + 1
F32, BF16 = jnp.float32, jnp.bfloat16


def ring(a, b, n):
    return min((a - b) % n, (b - a) % n)


def holders(m):
    z, x_hi = divmod(m, 2)
    x_lo, y = divmod(m, 8)
    zs = sorted(range(8), key=lambda v: (-ring(v, z, 8), v))
    ys = sorted(range(8), key=lambda v: (ring(v, y, 8), v))
    out = [0] * CHIPS
    for z_from, y_to in zip(zs, ys):
        for x_from in range(2):
            out[2 * z_from + x_from] = (x_lo if x_from == x_hi else 1 - x_lo) * 8 + y_to
    return out


HOLDERS = [holders(m) for m in range(CHIPS)]
ALONG_Z = [2 * z + x for x in range(2) for z in range(8)]
OVER_M = [[r * COL + 2 * m + k for m in ALONG_Z] for r in range(ROW) for k in range(2)]
SIBLING = [(i, i ^ 1) for i in range(ROW * COL)]


MIXED = [[r * COL + 2 * m for m in ALONG_Z] for r in range(ROW)] + [
    [r * COL + 2 * m + 1 for r in HOLDERS[m]] for m in range(CHIPS)
]


def to_column(core):
    return [(m * COL + 2 * s + core, HOLDERS[m][s] * COL + 2 * m + 1) for m in range(CHIPS) for s in range(CHIPS)]


TO_COLUMN_1 = to_column(1)
TO_COLUMN_0 = to_column(0) + [(i, i - 1) for i in range(1, ROW * COL, 2)]


AXES = ("row", "col")


def exchange(pieces, groups):
    return lax.all_to_all(pieces, AXES, 0, 0, tiled=True, axis_index_groups=groups)


def layer_norm(rows):
    mean = jnp.mean(rows, axis=-1, keepdims=True)
    centred = rows - mean
    var = jnp.mean(centred * centred, axis=-1, keepdims=True)
    return centred * lax.rsqrt(var + 1e-05)


def split(array):
    high = array.astype(BF16)
    return high, (array - high.astype(F32)).astype(BF16)


def dot(a, b):
    return lax.dot_general(a, b, (((1,), (0,)), ((), ())), preferred_element_type=F32)


def dot_t(a, b):
    return lax.dot_general(a, b, (((1,), (1,)), ((), ())), preferred_element_type=F32)


def left(high, low):
    return jnp.concatenate((high, low, high), 1)


def right(high, low, dim=1):
    return jnp.concatenate((high, high, low), dim)


def iota(shape, dim):
    return lax.broadcasted_iota(jnp.int32, shape, dim)


def pad_heads(rows, out):
    empty = jnp.zeros((SLOT - WIDTH, D), BF16)
    for h in range(HEADS):
        out[SLOT * h : SLOT * (h + 1), :] = jnp.concatenate((rows[WIDTH * h : WIDTH * (h + 1)], empty))


def fetch(sources, targets, sems):
    copies = [pltpu.make_async_copy(a, b, sems.at[i]) for i, (a, b) in enumerate(zip(sources, targets))]
    for copy in copies:
        copy.start()
    return copies


def prepare_kernel(
    singles, gain, w_out, w_gate, w_query, w_key, w_value,
    wt_h, wt_l, wo_h, wo_l, gate, singles_in, gain_in, held, gate_h, gate_l, out_h, out_l, sems,
):
    weights = (w_out, w_gate, w_query, w_key, w_value)
    copies = fetch((gain, *weights, singles), [gain_in.at[0]] + [held.at[i] for i in range(5)] + [singles_in], sems)
    copies[0].wait()
    copies[6].wait()
    normed = split(layer_norm(singles_in[...]) * gain_in[...])
    copies[1].wait()
    high, low = split(held[0])
    pad_heads(high, out_h)
    pad_heads(low, out_l)
    backs = fetch((out_h, out_l), (wo_h, wo_l), sems.at[pl.ds(8, 2)])
    copies[2].wait()
    high, low = split(held[1].T)
    pad_heads(high, gate_h)
    pad_heads(low, gate_l)
    gate[...] = jax.nn.sigmoid(dot_t(left(*normed), right(gate_h[...], gate_l[...])))
    for i in range(3):
        copies[i + 3].wait()
        at = pl.ds(i * D, D)
        wt_h[at], wt_l[at] = split(held[i + 2].T * gain_in[...])
    for copy in backs:
        copy.wait()


def in_hbm(*arrays):
    return [pltpu.with_memory_space_constraint(array, pltpu.HBM) for array in arrays]


def prepare(singles, gain, *weights):
    vmem, hbm = pl.BlockSpec(memory_space=pltpu.VMEM), pl.BlockSpec(memory_space=pl.ANY)
    return pl.pallas_call(
        prepare_kernel,
        out_shape=[pltpu.VMEM((3 * D, D), BF16)] * 2 + [pltpu.HBM((PAD, D), BF16)] * 2 + [pltpu.VMEM((SLICE, PAD), F32)],
        in_specs=[hbm] * 7,
        out_specs=[vmem] * 2 + [hbm] * 2 + [vmem],
        scratch_shapes=[pltpu.VMEM((SLICE, D), F32), pltpu.VMEM((1, D), F32), pltpu.VMEM((5, D, D), F32)]
        + [pltpu.VMEM((PAD, D), BF16)] * 4
        + [pltpu.SemaphoreType.DMA((10,))],
        compiler_params=pltpu.CompilerParams(vmem_limit_bytes=20 << 20),
        cost_estimate=pl.CostEstimate(flops=2 * 2304 * D * PAD, bytes_accessed=8 << 20, transcendentals=SLICE * D),
        name="prepare",
    )(*in_hbm(singles, gain, *weights))


def cut_kernel(core_ref, bias, theirs, half, sems):
    for copy in fetch((bias.at[:, :, 1 - core_ref[0]],), (half,), sems):
        copy.wait()
    for copy in fetch((half,), (theirs,), sems.at[pl.ds(1, 1)]):
        copy.wait()


def cut(core, bias):
    part = (HEADS, CHIPS, SLICE, LANES)
    hbm = pl.BlockSpec(memory_space=pl.ANY)
    return pl.pallas_call(
        cut_kernel,
        out_shape=pltpu.HBM(part, F32),
        in_specs=[pl.BlockSpec(memory_space=pltpu.SMEM), hbm],
        out_specs=hbm,
        scratch_shapes=[pltpu.VMEM(part, F32), pltpu.SemaphoreType.DMA((2,))],
        compiler_params=pltpu.CompilerParams(vmem_limit_bytes=20 << 20),
        cost_estimate=pl.CostEstimate(flops=0, bytes_accessed=4 << 20, transcendentals=0),
        name="cut",
    )(core.reshape(1), *in_hbm(bias.reshape(HEADS, CHIPS, 2, SLICE, LANES)))


def stage_kernel(core_ref, bias, other, held, sems):
    core = core_ref[0]
    sources, targets = [], []
    for x in range(2):
        chips = pl.ds(x * 8, 8)
        sources += [bias.at[:, :, x, core], other.at[:, :, x]]
        targets += [held.at[core, :, chips], held.at[1 - core, :, chips]]
    for copy in fetch(sources, targets, sems):
        copy.wait()


def stage(core, bias, other):
    hbm = pl.BlockSpec(memory_space=pl.ANY)
    return pl.pallas_call(
        stage_kernel,
        out_shape=pltpu.VMEM((2, HEADS, CHIPS, SLICE, LANES), F32),
        in_specs=[pl.BlockSpec(memory_space=pltpu.SMEM)] + [hbm] * 2,
        out_specs=pl.BlockSpec(memory_space=pltpu.VMEM),
        scratch_shapes=[pltpu.SemaphoreType.DMA((4,))],
        compiler_params=pltpu.CompilerParams(vmem_limit_bytes=20 << 20),
        cost_estimate=pl.CostEstimate(flops=0, bytes_accessed=4 << 20, transcendentals=0),
        name="stage",
    )(core.reshape(1), *in_hbm(bias.reshape(HEADS, 8, 2, 2, SLICE, LANES)), other.reshape(HEADS, 8, 2, SLICE, LANES))


def attend_kernel(core_ref, block, swapped, wt_h, wt_l, held, out):
    core = core_ref[0]
    first = core == 0
    own, given = block[...], swapped[...]
    q_rows = jnp.where(first, block[:, pl.ds(core, 1)], swapped[:, pl.ds(core, 1)]).reshape(TOKENS // 2, D)
    k_rows = jnp.where(first, given, own).reshape(TOKENS, D)
    q_norm = right(*split(layer_norm(q_rows)))
    k_norm = right(*split(layer_norm(k_rows)))
    half = TOKENS // 2
    queries = dot_t(left(wt_h[:D], wt_l[:D]), q_norm) * (1.0 / WIDTH**0.5)
    pairs = dot_t(left(wt_h[D:], wt_l[D:]), k_norm)
    slot = lax.shift_right_logical(iota((half, LANES), 1), 5)
    within = iota((half, LANES), 1) & (SLOT - 1)
    blank = jnp.zeros((SLOT - WIDTH, half), F32)
    blank_key = jnp.zeros((SLOT - WIDTH, TOKENS), F32)
    ones = jnp.where(iota((SLOT - WIDTH, TOKENS), 0) == TOTAL - WIDTH, 1.0, 0.0).astype(F32)

    def slots(rows, first, filler):
        parts = []
        for p in range(GROUP):
            parts += [rows[first + p * WIDTH : first + (p + 1) * WIDTH], filler]
        return jnp.concatenate(parts)

    for g in range(GROUPS):
        at = g * GROUP * WIDTH
        query_h, query_l = split(slots(queries, at, blank).T)
        key = right(*split(slots(pairs, at, blank_key)), 0)
        value_h, value_l = split(slots(pairs, D + at, ones))
        zero = jnp.zeros_like(query_h)
        lhs_h = jnp.concatenate([jnp.where(slot == p, query_h, zero) for p in range(GROUP)])
        lhs_l = jnp.concatenate([jnp.where(slot == p, query_l, zero) for p in range(GROUP)])
        scores = dot(left(lhs_h, lhs_l), key)
        tops, parts_h, parts_l = [], [], []
        for p in range(GROUP):
            h = g * GROUP + p
            added = jnp.concatenate([held[k, h].reshape(half, LANES) for k in range(2)], 1)
            one = scores[p * half : (p + 1) * half] + added
            top = jnp.max(one, axis=-1, keepdims=True)
            part_h, part_l = split(jnp.exp(one - top))
            tops.append(top)
            parts_h.append(part_h)
            parts_l.append(part_l)
        sums = dot_t(jnp.concatenate(parts_h), jnp.concatenate((value_h, value_l)))
        sums = sums[:, :LANES] + (sums[:, LANES:] + dot_t(jnp.concatenate(parts_l), value_h))
        tile = jnp.zeros((half, LANES), F32)
        for p in range(GROUP):
            one = jnp.where(within == TOP, tops[p], sums[p * half : (p + 1) * half])
            tile = jnp.where(slot == p, one, tile)
        out[:, :, g * LANES : (g + 1) * LANES] = tile.reshape(CHIPS, SLICE, LANES)


def attend(core, block, swapped, weights, staged):
    vmem = pl.BlockSpec(memory_space=pltpu.VMEM)
    shape = (CHIPS, 2, SLICE, D)
    return pl.pallas_call(
        attend_kernel,
        out_shape=jax.ShapeDtypeStruct((CHIPS, SLICE, PAD), F32),
        in_specs=[pl.BlockSpec(memory_space=pltpu.SMEM)] + [vmem] * 5,
        out_specs=vmem,
        compiler_params=pltpu.CompilerParams(vmem_limit_bytes=20 << 20),
        cost_estimate=pl.CostEstimate(flops=10**9, bytes_accessed=6 << 20, transcendentals=HEADS * 2**15),
        name="attend",
    )(core.reshape(1), block.reshape(shape), swapped.reshape(shape), *weights, staged)


def finish_kernel(parts, gate, wo_h, wo_l, singles, out):
    lane = iota((CHIPS * SLICE, LANES), 1)
    tops_at = lane - (lane & (SLOT - 1)) + TOP
    totals_at = tops_at[:SLICE] - TOP + TOTAL
    gated = []
    for g in range(GROUPS):
        cols = slice(g * LANES, (g + 1) * LANES)
        part = parts[:, :, cols]
        tops = jnp.take_along_axis(part.reshape(CHIPS * SLICE, LANES), tops_at, axis=1).reshape(CHIPS, SLICE, LANES)
        share = jnp.exp(tops - jnp.max(tops, axis=0, keepdims=True))
        sums = jnp.sum(part * share, axis=0)
        totals = jnp.take_along_axis(sums, totals_at, axis=1)
        gated.append(sums / totals * gate[:, cols])
    high, low = split(jnp.concatenate(gated, 1))
    both = dot(jnp.concatenate((high, low)), wo_h[...])
    out[...] = singles[...] + (both[:SLICE] + (both[SLICE:] + dot(high, wo_l[...])))


def finish(*args):
    return pl.pallas_call(
        finish_kernel,
        out_shape=jax.ShapeDtypeStruct((SLICE, D), F32),
        compiler_params=pltpu.CompilerParams(vmem_limit_bytes=4 << 20),
        cost_estimate=pl.CostEstimate(flops=6 * SLICE * PAD * D, bytes_accessed=2 << 20, transcendentals=CHIPS * SLICE * PAD),
        name="finish",
    )(*args)


def body(singles, norm_gain, w_query, w_key, w_value, w_gate, w_out, pair_bias):
    core = lax.axis_index("col") % 2
    moved = lax.ppermute(singles, AXES, TO_COLUMN_1)
    first = lax.ppermute(singles, AXES, TO_COLUMN_0)
    theirs = cut(core, pair_bias)
    moved, first, theirs = lax.optimization_barrier((moved, first, theirs))
    other = lax.ppermute(theirs, AXES, SIBLING)
    piece = jnp.where(core == 0, jnp.concatenate((singles, first)), jnp.concatenate((first, moved)))
    pieces, held = lax.optimization_barrier((jnp.broadcast_to(piece[None], (CHIPS, 2 * SLICE, D)), singles))
    wt_h, wt_l, wo_h, wo_l, gate = prepare(held, norm_gain, w_out, w_gate, w_query, w_key, w_value)
    block = exchange(pieces, MIXED)
    block, wt_h, wt_l, gate = lax.optimization_barrier((block, wt_h, wt_l, gate))
    swapped = lax.ppermute(block, AXES, SIBLING)
    message = attend(core, block, swapped, (wt_h, wt_l), stage(core, pair_bias, other))
    parts = exchange(message, OVER_M)
    return finish(parts, gate, wo_h, wo_l, singles)


def solution(mesh):
    return jax.shard_map(
        body,
        mesh=mesh,
        in_specs=(P(("row", "col"), None), P(), P(), P(), P(), P(), P(), P(None, "row", "col")),
        out_specs=P(("row", "col"), None),
        check_vma=False,
    )
```

```python
import jax
import jax.numpy as jnp
from jax import lax
from jax.experimental import pallas as pl
from jax.experimental.pallas import tpu as pltpu
from jax.sharding import PartitionSpec as P

ROW, COL, CHIPS = 16, 32, 16
SLICE = 8
D, HEADS, WIDTH = 384, 16, 24
TOKENS = 256
SLOT = 32
PAD = HEADS * SLOT
GROUP = 4
GROUPS = HEADS // GROUP
LANES = 128
TOTAL, TOP = WIDTH, WIDTH + 1
F32, BF16 = jnp.float32, jnp.bfloat16


def ring(a, b, n):
    return min((a - b) % n, (b - a) % n)


def holders(m):
    z, x_hi = divmod(m, 2)
    x_lo, y = divmod(m, 8)
    zs = sorted(range(8), key=lambda v: (-ring(v, z, 8), v))
    ys = sorted(range(8), key=lambda v: (ring(v, y, 8), v))
    out = [0] * CHIPS
    for z_from, y_to in zip(zs, ys):
        for x_from in range(2):
            out[2 * z_from + x_from] = (x_lo if x_from == x_hi else 1 - x_lo) * 8 + y_to
    return out


HOLDERS = [holders(m) for m in range(CHIPS)]
ALONG_Z = [2 * z + x for x in range(2) for z in range(8)]
OVER_M = [[r * COL + 2 * m + k for m in ALONG_Z] for r in range(ROW) for k in range(2)]
SIBLING = [(i, i ^ 1) for i in range(ROW * COL)]


MIXED = [[r * COL + 2 * m for m in ALONG_Z] for r in range(ROW)] + [
    [r * COL + 2 * m + 1 for r in HOLDERS[m]] for m in range(CHIPS)
]


def to_column(core):
    return [(m * COL + 2 * s + core, HOLDERS[m][s] * COL + 2 * m + 1) for m in range(CHIPS) for s in range(CHIPS)]


TO_COLUMN_1 = to_column(1)
TO_COLUMN_0 = to_column(0) + [(i, i - 1) for i in range(1, ROW * COL, 2)]


AXES = ("row", "col")


def exchange(pieces, groups):
    return lax.all_to_all(pieces, AXES, 0, 0, tiled=True, axis_index_groups=groups)


def layer_norm(rows):
    mean = jnp.mean(rows, axis=-1, keepdims=True)
    centred = rows - mean
    var = jnp.mean(centred * centred, axis=-1, keepdims=True)
    return centred * lax.rsqrt(var + 1e-05)


def split(array):
    high = array.astype(BF16)
    return high, (array - high.astype(F32)).astype(BF16)


def dot(a, b):
    return lax.dot_general(a, b, (((1,), (0,)), ((), ())), preferred_element_type=F32)


def dot_t(a, b):
    return lax.dot_general(a, b, (((1,), (1,)), ((), ())), preferred_element_type=F32)


def left(high, low):
    return jnp.concatenate((high, low, high), 1)


def right(high, low, dim=1):
    return jnp.concatenate((high, high, low), dim)


def iota(shape, dim):
    return lax.broadcasted_iota(jnp.int32, shape, dim)


def pad_heads(rows, out):
    empty = jnp.zeros((SLOT - WIDTH, D), BF16)
    for h in range(HEADS):
        out[SLOT * h : SLOT * (h + 1), :] = jnp.concatenate((rows[WIDTH * h : WIDTH * (h + 1)], empty))


def fetch(sources, targets, sems):
    copies = [pltpu.make_async_copy(a, b, sems.at[i]) for i, (a, b) in enumerate(zip(sources, targets))]
    for copy in copies:
        copy.start()
    return copies


def prepare_kernel(
    singles, gain, w_out, w_gate, w_query, w_key, w_value,
    wt_h, wt_l, wo_h, wo_l, gate, singles_in, gain_in, held, gate_h, gate_l, out_h, out_l, sems,
):
    weights = (w_out, w_gate, w_query, w_key, w_value)
    copies = fetch((gain, *weights, singles), [gain_in.at[0]] + [held.at[i] for i in range(5)] + [singles_in], sems)
    copies[0].wait()
    copies[6].wait()
    normed = split(layer_norm(singles_in[...]) * gain_in[...])
    copies[1].wait()
    high, low = split(held[0])
    pad_heads(high, out_h)
    pad_heads(low, out_l)
    backs = fetch((out_h, out_l), (wo_h, wo_l), sems.at[pl.ds(8, 2)])
    copies[2].wait()
    high, low = split(held[1].T)
    pad_heads(high, gate_h)
    pad_heads(low, gate_l)
    gate[...] = jax.nn.sigmoid(dot_t(left(*normed), right(gate_h[...], gate_l[...])))
    for i in range(3):
        copies[i + 3].wait()
        at = pl.ds(i * D, D)
        wt_h[at], wt_l[at] = split(held[i + 2].T * gain_in[...])
    for copy in backs:
        copy.wait()


def in_hbm(*arrays):
    return [pltpu.with_memory_space_constraint(array, pltpu.HBM) for array in arrays]


def prepare(singles, gain, *weights):
    vmem, hbm = pl.BlockSpec(memory_space=pltpu.VMEM), pl.BlockSpec(memory_space=pl.ANY)
    return pl.pallas_call(
        prepare_kernel,
        out_shape=[pltpu.VMEM((3 * D, D), BF16)] * 2 + [pltpu.HBM((PAD, D), BF16)] * 2 + [pltpu.VMEM((SLICE, PAD), F32)],
        in_specs=[hbm] * 7,
        out_specs=[vmem] * 2 + [hbm] * 2 + [vmem],
        scratch_shapes=[pltpu.VMEM((SLICE, D), F32), pltpu.VMEM((1, D), F32), pltpu.VMEM((5, D, D), F32)]
        + [pltpu.VMEM((PAD, D), BF16)] * 4
        + [pltpu.SemaphoreType.DMA((10,))],
        compiler_params=pltpu.CompilerParams(vmem_limit_bytes=20 << 20),
        cost_estimate=pl.CostEstimate(flops=2 * 2304 * D * PAD, bytes_accessed=8 << 20, transcendentals=SLICE * D),
        name="prepare",
    )(*in_hbm(singles, gain, *weights))


def cut_kernel(core_ref, bias, theirs, half, sems):
    parts = [pl.ds(i * GROUP, GROUP) for i in range(GROUPS)]
    ins = fetch([bias.at[p, :, 1 - core_ref[0]] for p in parts], [half.at[p] for p in parts], sems)
    outs = []
    for i, copy in enumerate(ins):
        copy.wait()
        outs += fetch((half.at[parts[i]],), (theirs.at[parts[i]],), sems.at[pl.ds(GROUPS + i, 1)])
    for copy in outs:
        copy.wait()


def cut(core, bias):
    part = (HEADS, CHIPS, SLICE, LANES)
    hbm = pl.BlockSpec(memory_space=pl.ANY)
    return pl.pallas_call(
        cut_kernel,
        out_shape=pltpu.HBM(part, F32),
        in_specs=[pl.BlockSpec(memory_space=pltpu.SMEM), hbm],
        out_specs=hbm,
        scratch_shapes=[pltpu.VMEM(part, F32), pltpu.SemaphoreType.DMA((2 * GROUPS,))],
        compiler_params=pltpu.CompilerParams(vmem_limit_bytes=20 << 20),
        cost_estimate=pl.CostEstimate(flops=0, bytes_accessed=4 << 20, transcendentals=0),
        name="cut",
    )(core.reshape(1), *in_hbm(bias.reshape(HEADS, CHIPS, 2, SLICE, LANES)))


def stage_kernel(core_ref, bias, other, held, sems):
    core = core_ref[0]
    sources, targets = [], []
    for x in range(2):
        chips = pl.ds(x * 8, 8)
        sources += [bias.at[:, :, x, core], other.at[:, :, x]]
        targets += [held.at[core, :, chips], held.at[1 - core, :, chips]]
    for copy in fetch(sources, targets, sems):
        copy.wait()


def stage(core, bias, other):
    hbm = pl.BlockSpec(memory_space=pl.ANY)
    return pl.pallas_call(
        stage_kernel,
        out_shape=pltpu.VMEM((2, HEADS, CHIPS, SLICE, LANES), F32),
        in_specs=[pl.BlockSpec(memory_space=pltpu.SMEM)] + [hbm] * 2,
        out_specs=pl.BlockSpec(memory_space=pltpu.VMEM),
        scratch_shapes=[pltpu.SemaphoreType.DMA((4,))],
        compiler_params=pltpu.CompilerParams(vmem_limit_bytes=20 << 20),
        cost_estimate=pl.CostEstimate(flops=0, bytes_accessed=4 << 20, transcendentals=0),
        name="stage",
    )(core.reshape(1), *in_hbm(bias.reshape(HEADS, 8, 2, 2, SLICE, LANES)), other.reshape(HEADS, 8, 2, SLICE, LANES))


def attend_kernel(core_ref, block, swapped, wt_h, wt_l, held, out):
    core = core_ref[0]
    first = core == 0
    own, given = block[...], swapped[...]
    q_rows = jnp.where(first, block[:, pl.ds(core, 1)], swapped[:, pl.ds(core, 1)]).reshape(TOKENS // 2, D)
    k_rows = jnp.where(first, given, own).reshape(TOKENS, D)
    q_norm = right(*split(layer_norm(q_rows)))
    k_norm = right(*split(layer_norm(k_rows)))
    half = TOKENS // 2
    queries = dot_t(left(wt_h[:D], wt_l[:D]), q_norm) * (1.0 / WIDTH**0.5)
    pairs = dot_t(left(wt_h[D:], wt_l[D:]), k_norm)
    slot = lax.shift_right_logical(iota((half, LANES), 1), 5)
    within = iota((half, LANES), 1) & (SLOT - 1)
    blank = jnp.zeros((SLOT - WIDTH, half), F32)
    blank_key = jnp.zeros((SLOT - WIDTH, TOKENS), F32)
    ones = jnp.where(iota((SLOT - WIDTH, TOKENS), 0) == TOTAL - WIDTH, 1.0, 0.0).astype(F32)

    def slots(rows, first, filler):
        parts = []
        for p in range(GROUP):
            parts += [rows[first + p * WIDTH : first + (p + 1) * WIDTH], filler]
        return jnp.concatenate(parts)

    for g in range(GROUPS):
        at = g * GROUP * WIDTH
        query_h, query_l = split(slots(queries, at, blank).T)
        key = right(*split(slots(pairs, at, blank_key)), 0)
        value_h, value_l = split(slots(pairs, D + at, ones))
        zero = jnp.zeros_like(query_h)
        lhs_h = jnp.concatenate([jnp.where(slot == p, query_h, zero) for p in range(GROUP)])
        lhs_l = jnp.concatenate([jnp.where(slot == p, query_l, zero) for p in range(GROUP)])
        scores = dot(left(lhs_h, lhs_l), key)
        tops, parts_h, parts_l = [], [], []
        for p in range(GROUP):
            h = g * GROUP + p
            added = jnp.concatenate([held[k, h].reshape(half, LANES) for k in range(2)], 1)
            one = scores[p * half : (p + 1) * half] + added
            top = jnp.max(one, axis=-1, keepdims=True)
            part_h, part_l = split(jnp.exp(one - top))
            tops.append(top)
            parts_h.append(part_h)
            parts_l.append(part_l)
        sums = dot_t(jnp.concatenate(parts_h), jnp.concatenate((value_h, value_l)))
        sums = sums[:, :LANES] + (sums[:, LANES:] + dot_t(jnp.concatenate(parts_l), value_h))
        tile = jnp.zeros((half, LANES), F32)
        for p in range(GROUP):
            one = jnp.where(within == TOP, tops[p], sums[p * half : (p + 1) * half])
            tile = jnp.where(slot == p, one, tile)
        out[:, :, g * LANES : (g + 1) * LANES] = tile.reshape(CHIPS, SLICE, LANES)


def attend(core, block, swapped, weights, staged):
    vmem = pl.BlockSpec(memory_space=pltpu.VMEM)
    shape = (CHIPS, 2, SLICE, D)
    return pl.pallas_call(
        attend_kernel,
        out_shape=jax.ShapeDtypeStruct((CHIPS, SLICE, PAD), F32),
        in_specs=[pl.BlockSpec(memory_space=pltpu.SMEM)] + [vmem] * 5,
        out_specs=vmem,
        compiler_params=pltpu.CompilerParams(vmem_limit_bytes=20 << 20),
        cost_estimate=pl.CostEstimate(flops=10**9, bytes_accessed=6 << 20, transcendentals=HEADS * 2**15),
        name="attend",
    )(core.reshape(1), block.reshape(shape), swapped.reshape(shape), *weights, staged)


def finish_kernel(parts, gate, wo_h, wo_l, singles, out):
    lane = iota((CHIPS * SLICE, LANES), 1)
    tops_at = lane - (lane & (SLOT - 1)) + TOP
    totals_at = tops_at[:SLICE] - TOP + TOTAL
    gated = []
    for g in range(GROUPS):
        cols = slice(g * LANES, (g + 1) * LANES)
        part = parts[:, :, cols]
        tops = jnp.take_along_axis(part.reshape(CHIPS * SLICE, LANES), tops_at, axis=1).reshape(CHIPS, SLICE, LANES)
        share = jnp.exp(tops - jnp.max(tops, axis=0, keepdims=True))
        sums = jnp.sum(part * share, axis=0)
        totals = jnp.take_along_axis(sums, totals_at, axis=1)
        gated.append(sums / totals * gate[:, cols])
    high, low = split(jnp.concatenate(gated, 1))
    both = dot(jnp.concatenate((high, low)), wo_h[...])
    out[...] = singles[...] + (both[:SLICE] + (both[SLICE:] + dot(high, wo_l[...])))


def finish(*args):
    return pl.pallas_call(
        finish_kernel,
        out_shape=jax.ShapeDtypeStruct((SLICE, D), F32),
        compiler_params=pltpu.CompilerParams(vmem_limit_bytes=4 << 20),
        cost_estimate=pl.CostEstimate(flops=6 * SLICE * PAD * D, bytes_accessed=2 << 20, transcendentals=CHIPS * SLICE * PAD),
        name="finish",
    )(*args)


def body(singles, norm_gain, w_query, w_key, w_value, w_gate, w_out, pair_bias):
    core = lax.axis_index("col") % 2
    moved = lax.ppermute(singles, AXES, TO_COLUMN_1)
    first = lax.ppermute(singles, AXES, TO_COLUMN_0)
    theirs = cut(core, pair_bias)
    moved, first, theirs = lax.optimization_barrier((moved, first, theirs))
    other = lax.ppermute(theirs, AXES, SIBLING)
    piece = jnp.where(core == 0, jnp.concatenate((singles, first)), jnp.concatenate((first, moved)))
    pieces, held = lax.optimization_barrier((jnp.broadcast_to(piece[None], (CHIPS, 2 * SLICE, D)), singles))
    wt_h, wt_l, wo_h, wo_l, gate = prepare(held, norm_gain, w_out, w_gate, w_query, w_key, w_value)
    block = exchange(pieces, MIXED)
    block, wt_h, wt_l, gate = lax.optimization_barrier((block, wt_h, wt_l, gate))
    swapped = lax.ppermute(block, AXES, SIBLING)
    message = attend(core, block, swapped, (wt_h, wt_l), stage(core, pair_bias, other))
    parts = exchange(message, OVER_M)
    return finish(parts, gate, wo_h, wo_l, singles)


def solution(mesh):
    return jax.shard_map(
        body,
        mesh=mesh,
        in_specs=(P(("row", "col"), None), P(), P(), P(), P(), P(), P(), P(None, "row", "col")),
        out_specs=P(("row", "col"), None),
        check_vma=False,
    )
```

```python
import jax
import jax.numpy as jnp
from jax import lax
from jax.experimental import pallas as pl
from jax.experimental.pallas import tpu as pltpu
from jax.sharding import PartitionSpec as P

ROW, COL, CHIPS = 16, 32, 16
SLICE = 8
D, HEADS, WIDTH = 384, 16, 24
TOKENS = 256
SLOT = 32
PAD = HEADS * SLOT
GROUP = 4
GROUPS = HEADS // GROUP
LANES = 128
TOTAL, TOP = WIDTH, WIDTH + 1
F32, BF16 = jnp.float32, jnp.bfloat16


def ring(a, b, n):
    return min((a - b) % n, (b - a) % n)


def holders(m):
    z, x_hi = divmod(m, 2)
    x_lo, y = divmod(m, 8)
    zs = sorted(range(8), key=lambda v: (-ring(v, z, 8), v))
    ys = sorted(range(8), key=lambda v: (ring(v, y, 8), v))
    out = [0] * CHIPS
    for z_from, y_to in zip(zs, ys):
        for x_from in range(2):
            out[2 * z_from + x_from] = (x_lo if x_from == x_hi else 1 - x_lo) * 8 + y_to
    return out


HOLDERS = [holders(m) for m in range(CHIPS)]
ALONG_Z = [2 * z + x for x in range(2) for z in range(8)]
OVER_M = [[r * COL + 2 * m + k for m in ALONG_Z] for r in range(ROW) for k in range(2)]
SIBLING = [(i, i ^ 1) for i in range(ROW * COL)]


MIXED = [[r * COL + 2 * m for m in ALONG_Z] for r in range(ROW)] + [
    [r * COL + 2 * m + 1 for r in HOLDERS[m]] for m in range(CHIPS)
]


def to_column(core):
    return [(m * COL + 2 * s + core, HOLDERS[m][s] * COL + 2 * m + 1) for m in range(CHIPS) for s in range(CHIPS)]


TO_COLUMN_1 = to_column(1)
TO_COLUMN_0 = to_column(0) + [(i, i - 1) for i in range(1, ROW * COL, 2)]


AXES = ("row", "col")


def exchange(pieces, groups):
    return lax.all_to_all(pieces, AXES, 0, 0, tiled=True, axis_index_groups=groups)


def layer_norm(rows):
    mean = jnp.mean(rows, axis=-1, keepdims=True)
    centred = rows - mean
    var = jnp.mean(centred * centred, axis=-1, keepdims=True)
    return centred * lax.rsqrt(var + 1e-05)


def split(array):
    high = array.astype(BF16)
    return high, (array - high.astype(F32)).astype(BF16)


def dot(a, b):
    return lax.dot_general(a, b, (((1,), (0,)), ((), ())), preferred_element_type=F32)


def dot_t(a, b):
    return lax.dot_general(a, b, (((1,), (1,)), ((), ())), preferred_element_type=F32)


def left(high, low):
    return jnp.concatenate((high, low, high), 1)


def right(high, low, dim=1):
    return jnp.concatenate((high, high, low), dim)


def iota(shape, dim):
    return lax.broadcasted_iota(jnp.int32, shape, dim)


def pad_heads(rows, out):
    empty = jnp.zeros((SLOT - WIDTH, D), BF16)
    for h in range(HEADS):
        out[SLOT * h : SLOT * (h + 1), :] = jnp.concatenate((rows[WIDTH * h : WIDTH * (h + 1)], empty))


def fetch(sources, targets, sems):
    copies = [pltpu.make_async_copy(a, b, sems.at[i]) for i, (a, b) in enumerate(zip(sources, targets))]
    for copy in copies:
        copy.start()
    return copies


def prepare_kernel(
    singles, gain, w_out, w_gate, w_query, w_key, w_value,
    wt_h, wt_l, wo_h, wo_l, gate, singles_in, gain_in, held, gate_h, gate_l, out_h, out_l, sems,
):
    weights = (w_out, w_gate, w_query, w_key, w_value)
    copies = fetch((gain, *weights, singles), [gain_in.at[0]] + [held.at[i] for i in range(5)] + [singles_in], sems)
    copies[0].wait()
    copies[6].wait()
    normed = split(layer_norm(singles_in[...]) * gain_in[...])
    copies[1].wait()
    high, low = split(held[0])
    pad_heads(high, out_h)
    pad_heads(low, out_l)
    backs = fetch((out_h, out_l), (wo_h, wo_l), sems.at[pl.ds(8, 2)])
    copies[2].wait()
    high, low = split(held[1].T)
    pad_heads(high, gate_h)
    pad_heads(low, gate_l)
    gate[...] = jax.nn.sigmoid(dot_t(left(*normed), right(gate_h[...], gate_l[...])))
    for i in range(3):
        copies[i + 3].wait()
        at = pl.ds(i * D, D)
        wt_h[at], wt_l[at] = split(held[i + 2].T * gain_in[...])
    for copy in backs:
        copy.wait()


def in_hbm(*arrays):
    return [pltpu.with_memory_space_constraint(array, pltpu.HBM) for array in arrays]


def prepare(singles, gain, *weights):
    vmem, hbm = pl.BlockSpec(memory_space=pltpu.VMEM), pl.BlockSpec(memory_space=pl.ANY)
    return pl.pallas_call(
        prepare_kernel,
        out_shape=[pltpu.VMEM((3 * D, D), BF16)] * 2 + [pltpu.HBM((PAD, D), BF16)] * 2 + [pltpu.VMEM((SLICE, PAD), F32)],
        in_specs=[hbm] * 7,
        out_specs=[vmem] * 2 + [hbm] * 2 + [vmem],
        scratch_shapes=[pltpu.VMEM((SLICE, D), F32), pltpu.VMEM((1, D), F32), pltpu.VMEM((5, D, D), F32)]
        + [pltpu.VMEM((PAD, D), BF16)] * 4
        + [pltpu.SemaphoreType.DMA((10,))],
        compiler_params=pltpu.CompilerParams(vmem_limit_bytes=20 << 20),
        cost_estimate=pl.CostEstimate(flops=2 * 2304 * D * PAD, bytes_accessed=8 << 20, transcendentals=SLICE * D),
        name="prepare",
    )(*in_hbm(singles, gain, *weights))


def cut_kernel(core_ref, bias, theirs, half, sems):
    parts = [pl.ds(i * GROUP, GROUP) for i in range(GROUPS)]
    ins = fetch([bias.at[p, :, 1 - core_ref[0]] for p in parts], [half.at[p] for p in parts], sems)
    outs = []
    for i, copy in enumerate(ins):
        copy.wait()
        outs += fetch((half.at[parts[i]],), (theirs.at[parts[i]],), sems.at[pl.ds(GROUPS + i, 1)])
    for copy in outs:
        copy.wait()


def cut(core, bias):
    part = (HEADS, CHIPS, SLICE, LANES)
    hbm = pl.BlockSpec(memory_space=pl.ANY)
    return pl.pallas_call(
        cut_kernel,
        out_shape=pltpu.HBM(part, F32),
        in_specs=[pl.BlockSpec(memory_space=pltpu.SMEM), hbm],
        out_specs=hbm,
        scratch_shapes=[pltpu.VMEM(part, F32), pltpu.SemaphoreType.DMA((2 * GROUPS,))],
        compiler_params=pltpu.CompilerParams(vmem_limit_bytes=20 << 20),
        cost_estimate=pl.CostEstimate(flops=0, bytes_accessed=4 << 20, transcendentals=0),
        name="cut",
    )(core.reshape(1), *in_hbm(bias.reshape(HEADS, CHIPS, 2, SLICE, LANES)))


def stage_kernel(core_ref, bias, other, held, sems):
    core = core_ref[0]
    sources, targets = [], []
    for x in range(2):
        chips = pl.ds(x * 8, 8)
        sources += [bias.at[:, :, x, core], other.at[:, :, x]]
        targets += [held.at[core, :, chips], held.at[1 - core, :, chips]]
    for copy in fetch(sources, targets, sems):
        copy.wait()


def stage(core, bias, other):
    hbm = pl.BlockSpec(memory_space=pl.ANY)
    return pl.pallas_call(
        stage_kernel,
        out_shape=pltpu.VMEM((2, HEADS, CHIPS, SLICE, LANES), F32),
        in_specs=[pl.BlockSpec(memory_space=pltpu.SMEM)] + [hbm] * 2,
        out_specs=pl.BlockSpec(memory_space=pltpu.VMEM),
        scratch_shapes=[pltpu.SemaphoreType.DMA((4,))],
        compiler_params=pltpu.CompilerParams(vmem_limit_bytes=20 << 20),
        cost_estimate=pl.CostEstimate(flops=0, bytes_accessed=4 << 20, transcendentals=0),
        name="stage",
    )(core.reshape(1), *in_hbm(bias.reshape(HEADS, 8, 2, 2, SLICE, LANES)), other.reshape(HEADS, 8, 2, SLICE, LANES))


def attend_kernel(core_ref, block, swapped, wt_h, wt_l, held, out):
    core = core_ref[0]
    first = core == 0
    own, given = block[...], swapped[...]
    q_rows = jnp.where(first, block[:, pl.ds(core, 1)], swapped[:, pl.ds(core, 1)]).reshape(TOKENS // 2, D)
    k_rows = jnp.where(first, given, own).reshape(TOKENS, D)
    q_norm = right(*split(layer_norm(q_rows)))
    k_norm = right(*split(layer_norm(k_rows)))
    half = TOKENS // 2
    queries = dot_t(left(wt_h[:D], wt_l[:D]), q_norm) * (1.0 / WIDTH**0.5)
    pairs = dot_t(left(wt_h[D:], wt_l[D:]), k_norm)
    slot = lax.shift_right_logical(iota((half, LANES), 1), 5)
    within = iota((half, LANES), 1) & (SLOT - 1)
    blank = jnp.zeros((SLOT - WIDTH, half), F32)
    blank_key = jnp.zeros((SLOT - WIDTH, TOKENS), F32)
    ones = jnp.where(iota((SLOT - WIDTH, TOKENS), 0) == TOTAL - WIDTH, 1.0, 0.0).astype(F32)

    def slots(rows, first, filler):
        parts = []
        for p in range(GROUP):
            parts += [rows[first + p * WIDTH : first + (p + 1) * WIDTH], filler]
        return jnp.concatenate(parts)

    for g in range(GROUPS):
        at = g * GROUP * WIDTH
        query_h, query_l = split(slots(queries, at, blank).T)
        key = right(*split(slots(pairs, at, blank_key)), 0)
        value_h, value_l = split(slots(pairs, D + at, ones))
        zero = jnp.zeros_like(query_h)
        lhs_h = jnp.concatenate([jnp.where(slot == p, query_h, zero) for p in range(GROUP)])
        lhs_l = jnp.concatenate([jnp.where(slot == p, query_l, zero) for p in range(GROUP)])
        scores = dot(left(lhs_h, lhs_l), key)
        tops, parts_h, parts_l = [], [], []
        for p in range(GROUP):
            h = g * GROUP + p
            added = jnp.concatenate([held[k, h].reshape(half, LANES) for k in range(2)], 1)
            one = scores[p * half : (p + 1) * half] + added
            top = jnp.max(one, axis=-1, keepdims=True)
            part_h, part_l = split(jnp.exp(one - top))
            tops.append(top)
            parts_h.append(part_h)
            parts_l.append(part_l)
        sums = dot_t(jnp.concatenate(parts_h), jnp.concatenate((value_h, value_l)))
        sums = sums[:, :LANES] + (sums[:, LANES:] + dot_t(jnp.concatenate(parts_l), value_h))
        tile = jnp.zeros((half, LANES), F32)
        for p in range(GROUP):
            one = jnp.where(within == TOP, tops[p], sums[p * half : (p + 1) * half])
            tile = jnp.where(slot == p, one, tile)
        out[:, :, g * LANES : (g + 1) * LANES] = tile.reshape(CHIPS, SLICE, LANES)


def attend(core, block, swapped, weights, staged):
    vmem = pl.BlockSpec(memory_space=pltpu.VMEM)
    shape = (CHIPS, 2, SLICE, D)
    return pl.pallas_call(
        attend_kernel,
        out_shape=jax.ShapeDtypeStruct((CHIPS, SLICE, PAD), F32),
        in_specs=[pl.BlockSpec(memory_space=pltpu.SMEM)] + [vmem] * 5,
        out_specs=vmem,
        compiler_params=pltpu.CompilerParams(vmem_limit_bytes=20 << 20),
        cost_estimate=pl.CostEstimate(flops=10**9, bytes_accessed=6 << 20, transcendentals=HEADS * 2**15),
        name="attend",
    )(core.reshape(1), block.reshape(shape), swapped.reshape(shape), *weights, staged)


def finish_kernel(parts, gate, wo_h, wo_l, singles, out):
    lane = iota((CHIPS * SLICE, LANES), 1)
    tops_at = lane - (lane & (SLOT - 1)) + TOP
    totals_at = tops_at[:SLICE] - TOP + TOTAL
    gated = []
    for g in range(GROUPS):
        cols = slice(g * LANES, (g + 1) * LANES)
        part = parts[:, :, cols]
        tops = jnp.take_along_axis(part.reshape(CHIPS * SLICE, LANES), tops_at, axis=1).reshape(CHIPS, SLICE, LANES)
        share = jnp.exp(tops - jnp.max(tops, axis=0, keepdims=True))
        sums = jnp.sum(part * share, axis=0)
        totals = jnp.take_along_axis(sums, totals_at, axis=1)
        gated.append(sums / totals * gate[:, cols])
    high, low = split(jnp.concatenate(gated, 1))
    both = dot(jnp.concatenate((high, low)), wo_h[...])
    out[...] = singles[...] + (both[:SLICE] + (both[SLICE:] + dot(high, wo_l[...])))


def finish(*args):
    return pl.pallas_call(
        finish_kernel,
        out_shape=jax.ShapeDtypeStruct((SLICE, D), F32),
        compiler_params=pltpu.CompilerParams(vmem_limit_bytes=4 << 20),
        cost_estimate=pl.CostEstimate(flops=6 * SLICE * PAD * D, bytes_accessed=2 << 20, transcendentals=CHIPS * SLICE * PAD),
        name="finish",
    )(*args)


def body(singles, norm_gain, w_query, w_key, w_value, w_gate, w_out, pair_bias):
    core = lax.axis_index("col") % 2
    moved = lax.ppermute(singles, AXES, TO_COLUMN_1)
    first = lax.ppermute(singles, AXES, TO_COLUMN_0)
    theirs = cut(core, pair_bias)
    other = lax.ppermute(theirs, AXES, SIBLING)
    piece = jnp.where(core == 0, jnp.concatenate((singles, first)), jnp.concatenate((first, moved)))
    pieces, held = lax.optimization_barrier((jnp.broadcast_to(piece[None], (CHIPS, 2 * SLICE, D)), singles))
    wt_h, wt_l, wo_h, wo_l, gate = prepare(held, norm_gain, w_out, w_gate, w_query, w_key, w_value)
    block = exchange(pieces, MIXED)
    block, wt_h, wt_l, gate = lax.optimization_barrier((block, wt_h, wt_l, gate))
    swapped = lax.ppermute(block, AXES, SIBLING)
    message = attend(core, block, swapped, (wt_h, wt_l), stage(core, pair_bias, other))
    parts = exchange(message, OVER_M)
    return finish(parts, gate, wo_h, wo_l, singles)


def solution(mesh):
    return jax.shard_map(
        body,
        mesh=mesh,
        in_specs=(P(("row", "col"), None), P(), P(), P(), P(), P(), P(), P(None, "row", "col")),
        out_specs=P(("row", "col"), None),
        check_vma=False,
    )
```
